32 devices in a mesh: dp: 4 (over y, x), expert: 8 (over z, core).
Axes of the slice: x: 2, y: 2, z: 4, core: 2. Of those that a mesh axis runs over, the one named last changes fastest.
Arguments:
- tokens: bfloat16 [2048, 2048], P(('dp', 'expert')), may hold values from -6 to 6
- expert_ids: int32 [2048, 8], P(('dp', 'expert')), may hold values from 0 to 31, all different within a row; in each aligned block of 64 rows (0 to 63, 64 to 127, ...) at most 24 rows name the same one
- gate_fixed: int32 [2048, 8], P(('dp', 'expert')), may hold values from 1 to 65535
- scorer_id: int32 [128], P(('dp', 'expert')), may hold values from 0 to 1
- direction_tags: bfloat16 [2, 2048], replicated, may hold values from -6 to 6
- w_gate: bfloat16 [32, 2048, 512], P('expert'), may hold values from -0.125 to 0.125
- w_up: bfloat16 [32, 2048, 512], P('expert'), may hold values from -0.125 to 0.125
- w_down: bfloat16 [32, 512, 2048], P('expert'), may hold values from -0.25 to 0.25
- score_head: float32 [2048], replicated, may hold values from -0.125 to 0.125
Outputs:
- mixed: bfloat16 [2048, 2048], P(('dp', 'expert'))
- pair_score: float32 [128], P(('dp', 'expert'))
The draws below stay inside these ranges and needn't reach their ends.
Inputs may be any that keep to these rules, and one draw needn't show every extreme that they name: `expert_ids`: each row names 8 different experts. Among the rows of one device no expert is named by more than 24 rows, and in some devices' rows an expert is named by exactly 24.
All inputs are finite; a program needn't handle non-finite values.
Results may differ from the reference program's by a relative error of at most 0.04.
Values may be sent and summed in bfloat16 or wider, within the bound.
No kernel may reach another device: no remote copies, remote signals or barrier semaphores. Data moves between devices by JAX's collectives and lax.ppermute only.
A program may use at most 64 MiB of HBM per device.

```python
import math
import jax
import jax.numpy as jnp
import numpy as np
from jax import lax

D = 2048
FF = 512
EXPERTS = 32
TOP = 8
SEQ_LEN = 16
TOK_DEV = 64
MOST = 24
TOKENS = 2048
SEQS = 128


def plant(result, own_key, smallest, top_value):
    longest = result.shape.index(max(result.shape))
    spots = []
    for shift in (0, 1):
        where = [jax.random.randint(jax.random.fold_in(own_key, axis), (), 0, length) for axis, length in enumerate(result.shape)]
        where[longest] = (where[longest] + shift) % result.shape[longest]
        spots.append(tuple(where))
    return result.at[spots[0]].set(smallest).at[spots[1]].set(top_value)


def block_scale(stream_key, shape, split, least, largest):
    def one(position, shards_of):
        steps = jax.random.uniform(jax.random.fold_in(jax.random.fold_in(stream_key, 6), position), (shards_of,), jnp.float32, least / len(split), largest / len(split))
        return jnp.repeat(jnp.exp(steps), shape[position] // shards_of).reshape((-1,) + (1,) * (len(shape) - position - 1))

    factor_of = one(*split[0])
    for cut in split[1:]:
        factor_of = factor_of * one(*cut)
    return factor_of


def shared_out(own_key, own, number, rows, count, top, bound, slope):
    sequence = jax.random.permutation(own_key, count)
    crowded, ordinary = shares(count, rows * top, bound, slope, True), shares(count, rows * top, bound, slope, False)
    places = jnp.arange(count)

    def named(tallies, rotation):
        used = int((tallies > 0).sum())
        fixed = max(1, used // 4)
        passed = fixed + (places - fixed + rotation * (used - fixed)) % max(1, count - fixed)
        return jnp.zeros((count,), jnp.int32).at[sequence[jnp.where(places < fixed, places, passed)]].set(jnp.asarray(tallies, jnp.int32))

    tallies = jnp.where(number % 4 == 0, named(crowded, number // 4), named(ordinary, number - number // 4 - 1))
    mixed = jax.random.permutation(jax.random.fold_in(own, 3), count)
    giver, sink = mixed[0:count // 2 * 2:2], mixed[1:count // 2 * 2:2]
    room = jnp.minimum(tallies[giver] - 1, bound - tallies[sink]) // 2
    room = jnp.where((giver == sequence[0]) | (sink == sequence[0]) | (tallies[sink] == 0), 0, jnp.maximum(room, 0))
    passed = jax.random.randint(jax.random.fold_in(own, 4), (count // 2,), 0, 1 << 20) % (room + 1)
    tallies = tallies.at[giver].add(-passed).at[sink].add(passed)
    labels = jnp.searchsorted(jnp.cumsum(tallies), jnp.arange(rows * top), side="right").astype(jnp.int32)
    table = labels.reshape(top, rows).T
    table = table[jax.random.permutation(jax.random.fold_in(own, 1), rows)]
    rotation = jax.random.randint(jax.random.fold_in(own, 2), (rows, 1), 0, top)
    return jnp.take_along_axis(table, (jnp.arange(top)[None, :] + rotation) % top, axis=1)


def shares(number_of, total, most, slope, full):
    weights = [(1 << 20) // math.isqrt(standing ** slope) + 1 for standing in range(1, number_of + 1)]
    largest = most if full else min(most, max(-(-total // number_of), total * weights[0] // sum(weights)))
    least = 1 if total - largest >= number_of - 1 else 0
    counts, rest = [largest] + [least] * (number_of - 1), total - largest - least * (number_of - 1)
    while rest > 0:
        free = [i for i in range(1, number_of) if counts[i] < largest] or [i for i in range(1, number_of) if counts[i] < most]
        pool, remaining = sum([weights[i] for i in free]), rest
        for i in free:
            addition = min(most - counts[i], max(1, remaining * weights[i] // pool), rest)
            counts[i] = counts[i] + addition
            rest = rest - addition
    return np.array(counts)


def normal_values(stream_key, dims, width, bound, shards=(), kind=jnp.bfloat16):
    array = width * jax.random.normal(stream_key, dims, jnp.float32)
    if shards:
        array = array * block_scale(stream_key, dims, shards, -0.22, 0.18)
    return jnp.clip(array, -bound, bound).astype(kind)


def setup_inputs(seed: int = 0) -> dict:
    splits = jax.random.split(jax.random.key(seed), 10)
    tokens = normal_values(splits[0], (TOKENS, D), 1.0, 6.0, ((0, 32),))
    expert_ids_keys = jax.random.split(jax.random.fold_in(splits[1], 1), TOKENS // TOK_DEV)
    expert_ids_turns = jax.random.permutation(jax.random.fold_in(splits[1], 3), TOKENS // TOK_DEV)
    expert_ids = jax.vmap(lambda own, number: shared_out(jax.random.fold_in(splits[1], 2), own, number, TOK_DEV, EXPERTS, TOP, MOST, 2))(expert_ids_keys, expert_ids_turns).reshape((TOKENS, TOP))
    gate_fixed = plant(jax.random.randint(splits[2], (TOKENS, TOP), 1, 65536), jax.random.fold_in(splits[2], 1), 1, 65535).astype(jnp.int32)
    scorer_id = plant(jax.random.randint(splits[3], (SEQS,), 0, 2), jax.random.fold_in(splits[3], 1), 0, 1).astype(jnp.int32)
    direction_tags = normal_values(splits[4], (2, D), 1.0, 6.0)
    w_gate = normal_values(splits[5], (EXPERTS, D, FF), D ** -0.5, 0.125, ((0, 8),))
    w_up = normal_values(splits[6], (EXPERTS, D, FF), D ** -0.5, 0.125, ((0, 8),))
    w_down = normal_values(splits[7], (EXPERTS, FF, D), FF ** -0.5, 0.25, ((0, 8),))
    score_head = normal_values(splits[8], (D,), D ** -0.5, 0.125, (), jnp.float32)
    return dict(tokens=tokens, expert_ids=expert_ids, gate_fixed=gate_fixed, scorer_id=scorer_id, direction_tags=direction_tags, w_gate=w_gate, w_up=w_up, w_down=w_down, score_head=score_head)


def reference(tokens, expert_ids, gate_fixed, scorer_id, direction_tags, w_gate, w_up, w_down, score_head):
    tok_scorer = jnp.repeat(scorer_id, SEQ_LEN)
    tag_rows = direction_tags.astype(jnp.float32)[tok_scorer]
    inputs = (tokens.astype(jnp.float32) + tag_rows).astype(jnp.bfloat16)
    fixed_val = gate_fixed.astype(jnp.float32)
    weight = fixed_val / jnp.sum(fixed_val, axis=1, keepdims=True)
    blocks = TOKENS // TOK_DEV
    flat_ids = expert_ids.reshape(blocks, TOK_DEV * TOP)
    onehot = (flat_ids[:, :, None] == jnp.arange(EXPERTS, dtype=jnp.int32)[None, None, :]).astype(jnp.int32)
    rank_in = jnp.sum(jnp.cumsum(onehot, axis=1) * onehot, axis=2) - 1
    block_index = jnp.arange(blocks, dtype=jnp.int32)[:, None]
    slot_index = block_index * MOST + rank_in
    token_of = block_index * TOK_DEV + jnp.arange(TOK_DEV * TOP, dtype=jnp.int32)[None, :] // TOP
    capacity = blocks * MOST
    slot_table = jnp.zeros((EXPERTS, capacity), jnp.int32).at[flat_ids, slot_index].set(token_of)
    slot_weight = jnp.zeros((EXPERTS, capacity), jnp.float32).at[flat_ids, slot_index].set(weight.reshape(blocks, TOK_DEV * TOP))

    def scan_step(summed, expert_index):
        picked = slot_table[expert_index]
        row_block = inputs[picked]
        gate_proj = jnp.dot(row_block, w_gate[expert_index], preferred_element_type=jnp.float32)
        up_proj = jnp.dot(row_block, w_up[expert_index], preferred_element_type=jnp.float32)
        hidden = (jax.nn.silu(gate_proj) * up_proj).astype(jnp.bfloat16)
        down_out = jnp.dot(hidden, w_down[expert_index], preferred_element_type=jnp.float32)
        expert_out = (slot_weight[expert_index][:, None] * down_out).astype(jnp.bfloat16)
        return summed.at[picked].add(expert_out.astype(jnp.float32)), None

    summed, _ = lax.scan(scan_step, jnp.zeros((TOKENS, D), jnp.float32), jnp.arange(EXPERTS, dtype=jnp.int32))
    mixed = summed.astype(jnp.bfloat16)
    token_score = jnp.dot(mixed.astype(jnp.float32), score_head, precision=lax.Precision.HIGHEST)
    seq_score = token_score.reshape(SEQS, SEQ_LEN).sum(axis=1)
    partner = jnp.roll(seq_score, SEQS // 2)
    pair_score = jnp.abs(seq_score - partner) + 0.5 * (seq_score + partner)
    return mixed, pair_score
```

```python
import functools

import jax
import jax.numpy as jnp
from jax import lax
from jax.experimental import pallas as pl
from jax.experimental.pallas import tpu as pltpu
from jax.sharding import PartitionSpec as P

SEQ_LEN = 16
MOST = 24
META = 128
MIB = 1 << 20

VMEM = pl.BlockSpec(memory_space=pltpu.VMEM)
SMEM = pl.BlockSpec(memory_space=pltpu.SMEM)
ANY = pl.BlockSpec(memory_space=pl.ANY)


def prep_kernel(experts, tok_ref, ids_ref, gate_ref, scorer_ref, tags_ref, out_ref):
    rows, width = tok_ref.shape
    for s in range(rows // SEQ_LEN):
        span = pl.ds(s * SEQ_LEN, SEQ_LEN)
        tag = jnp.where(scorer_ref[s] == 1, tags_ref[1:2, :], tags_ref[0:1, :]).astype(jnp.float32)
        out_ref[span, 0:width] = (tok_ref[span, :].astype(jnp.float32) + tag).astype(jnp.bfloat16)
    fixed = gate_ref[...].astype(jnp.float32)
    weight = fixed / jnp.sum(fixed, axis=1, keepdims=True)
    high = weight.astype(jnp.bfloat16).astype(jnp.float32)
    low = weight - high
    ids = ids_ref[...]
    lane = lax.broadcasted_iota(jnp.int32, (rows, META), 1)
    meta = jnp.zeros((rows, META), jnp.float32)
    for k in range(ids.shape[1]):
        one = ids[:, k : k + 1]
        meta = meta + jnp.where(lane == one, high[:, k : k + 1], 0.0)
        meta = meta + jnp.where(lane == one + experts, low[:, k : k + 1], 0.0)
    out_ref[:, width : width + META] = meta.astype(jnp.bfloat16)


def pick_rows(meta, first, per_device, experts):
    rows = meta.shape[0]
    room = 2 * MOST
    lane = lax.broadcasted_iota(jnp.int32, meta.shape, 1)
    routed = (meta > 0) & (lane < experts)
    row = lax.broadcasted_iota(jnp.int32, (rows, rows), 0)
    col = lax.broadcasted_iota(jnp.int32, (rows, rows), 1)
    earlier = (row > col).astype(jnp.bfloat16)
    rank = jnp.dot(earlier, routed.astype(jnp.bfloat16), preferred_element_type=jnp.float32)
    rank = jnp.where(routed, rank, -1.0)
    slot = lax.broadcasted_iota(jnp.int32, (rows, per_device * room), 1)
    hit = jnp.zeros((rows, per_device * room), jnp.bool_)
    for e in range(per_device):
        mine = jnp.max(jnp.where(lane == first + e, rank, -1.0), axis=1, keepdims=True).astype(jnp.int32)
        hit = hit | ((mine >= 0) & (slot == mine + e * room))
    return hit.astype(jnp.float32).astype(jnp.bfloat16)


def ffn_kernel(groups, experts, *refs):
    total = sum(a + b for a, b in groups)
    x_refs, refs = refs[:total], refs[total:]
    wg_hbm, wu_hbm, wd_hbm, same_ref, other_ref, wg, wu, wd, g_ref, pick_ref, o_ref, sems = refs
    per_device, width, ff = wg_hbm.shape
    room = 2 * MOST
    first = lax.axis_index("expert") * per_device
    copies = []
    for e in range(per_device):
        for j, (src, dst) in enumerate(((wg_hbm, wg), (wu_hbm, wu), (wd_hbm, wd))):
            copy = pltpu.make_async_copy(src.at[e], dst.at[e], sems.at[e, j])
            copy.start()
            copies.append(copy)
    at = 0
    for k, (a, b) in enumerate(groups):
        halves = []
        for n in (a, b):
            value = x_refs[at][...]
            for i in range(1, n):
                value = value + x_refs[at + i][...]
            at += n
            halves.append(value)
        x = jnp.concatenate(halves, axis=0)
        pick = pick_rows(x[:, width:].astype(jnp.float32), first, per_device, experts)
        pick_ref[k] = pick
        picked = lax.dot_general(pick, x, (((0,), (0,)), ((), ())), preferred_element_type=jnp.float32)
        picked = picked.astype(jnp.bfloat16)
        for e in range(per_device):
            g_ref[e, k * room : (k + 1) * room, :] = picked[e * room : (e + 1) * room, :]
    lane = lax.broadcasted_iota(jnp.int32, (len(groups) * room, META), 1)
    for e in range(per_device):
        x = g_ref[e, :, 0:width]
        meta = g_ref[e, :, width:].astype(jnp.float32)
        mine = (lane == first + e) | (lane == first + e + experts)
        weight = jnp.sum(jnp.where(mine, meta, 0.0), axis=1, keepdims=True)
        copies[3 * e].wait()
        gate = jnp.dot(x, wg[e], preferred_element_type=jnp.float32)
        copies[3 * e + 1].wait()
        up = jnp.dot(x, wu[e], preferred_element_type=jnp.float32)
        hidden = (gate / (1.0 + jnp.exp(-gate)) * up * weight).astype(jnp.bfloat16)
        copies[3 * e + 2].wait()
        out = jnp.dot(hidden, wd[e], preferred_element_type=jnp.float32).astype(jnp.bfloat16)
        for k in range(len(groups)):
            o_ref[k, e * room : (e + 1) * room, :] = out[k * room : (k + 1) * room, :]
    for k in range(len(groups)):
        rows = jnp.dot(pick_ref[k], o_ref[k], preferred_element_type=jnp.float32).astype(jnp.bfloat16)
        half = rows.shape[0] // 2
        same_ref[k] = rows[:half]
        other_ref[k] = rows[half:]


def ffn(groups, experts, xs, w_gate, w_up, w_down):
    per_device, width, ff = w_gate.shape
    rows = xs[0].shape[0]
    chips = len(groups)
    room = 2 * MOST
    out = jax.ShapeDtypeStruct((chips, rows, width), jnp.bfloat16)
    return pl.pallas_call(
        functools.partial(ffn_kernel, groups, experts),
        out_shape=(out, out),
        in_specs=[VMEM] * len(xs) + [ANY] * 3,
        out_specs=(VMEM, VMEM),
        scratch_shapes=[
            pltpu.VMEM((per_device, width, ff), jnp.bfloat16),
            pltpu.VMEM((per_device, width, ff), jnp.bfloat16),
            pltpu.VMEM((per_device, ff, width), jnp.bfloat16),
            pltpu.VMEM((per_device, chips * room, width + META), jnp.bfloat16),
            pltpu.VMEM((chips, 2 * rows, per_device * room), jnp.bfloat16),
            pltpu.VMEM((chips, per_device * room, width), jnp.bfloat16),
            pltpu.SemaphoreType.DMA((per_device, 3)),
        ],
        compiler_params=pltpu.CompilerParams(vmem_limit_bytes=56 * MIB),
        cost_estimate=pl.CostEstimate(
            flops=6 * per_device * chips * room * width * ff,
            bytes_accessed=6 * per_device * width * ff,
            transcendentals=0,
        ),
        name="ffn",
    )(*xs, w_gate, w_up, w_down)


def finish_kernel(n_parts, *refs):
    parts, head_ref, mixed_ref, score_ref = refs[:n_parts], *refs[n_parts:]
    rows = mixed_ref.shape[0]
    total = parts[0][...].astype(jnp.float32)
    for part in parts[1:]:
        total = total + part[...].astype(jnp.float32)
    mixed = total.astype(jnp.bfloat16)
    mixed_ref[...] = mixed
    scored = mixed.astype(jnp.float32) * head_ref[...]
    for s in range(rows // SEQ_LEN):
        score_ref[s] = jnp.sum(scored[s * SEQ_LEN : (s + 1) * SEQ_LEN, :])


def send(x, route):
    return lax.ppermute(x, "expert", route)


def body(tokens, expert_ids, gate_fixed, scorer_id, direction_tags, w_gate, w_up, w_down, score_head):
    devices = lax.axis_size("expert")
    chips = devices // 2
    experts = w_gate.shape[0] * devices
    rows, width = tokens.shape
    x = pl.pallas_call(
        functools.partial(prep_kernel, experts),
        out_shape=jax.ShapeDtypeStruct((rows, width + META), jnp.bfloat16),
        in_specs=[VMEM, VMEM, VMEM, SMEM, VMEM],
        out_specs=VMEM,
        name="prep",
    )(tokens, expert_ids, gate_fixed, scorer_id, direction_tags)

    def exchange(block, k):
        return send(block, [(d, d ^ (2 * k)) for d in range(devices)])

    def core_swap(block):
        return send(block, [(d, d ^ 1) for d in range(devices)])

    hybrid = chips == 4
    middle = [(2 * a + c, 2 * b + c) for a, b in ((1, 2), (2, 1)) for c in (0, 1)]
    outward = [(2 * a + c, 2 * b + c) for a, b in ((1, 0), (2, 3)) for c in (0, 1)]
    inward = [(b, a) for a, b in outward]

    if hybrid:
        far = exchange(x, 2)
        near = exchange(x, 1)
        mid = send(x, middle)
        last = send(far, outward)
        held = [[x], [near], [far], [mid, last]]
    else:
        held = [[x]] + [[exchange(x, k)] for k in range(1, chips)]
    groups, xs = [], []
    for blocks in held:
        one = [core_swap(b) for b in blocks]
        groups.append((len(blocks), len(one)))
        xs += blocks + one
    same, other = ffn(tuple(groups), experts, xs, w_gate, w_up, w_down)
    swapped = core_swap(other)
    summed = (same.astype(jnp.float32) + swapped.astype(jnp.float32)).astype(jnp.bfloat16)
    if hybrid:
        early = send(summed[3], inward)
        far_sum = (summed[2].astype(jnp.float32) + early.astype(jnp.float32)).astype(jnp.bfloat16)
        parts = [summed[0], exchange(summed[1], 1), send(summed[3], middle), exchange(far_sum, 2)]
    else:
        parts = [summed[0]] + [exchange(summed[k], k) for k in range(1, chips)]
    mixed, seq_score = pl.pallas_call(
        functools.partial(finish_kernel, len(parts)),
        out_shape=(
            jax.ShapeDtypeStruct((rows, width), jnp.bfloat16),
            jax.ShapeDtypeStruct((rows // SEQ_LEN,), jnp.float32),
        ),
        in_specs=[VMEM] * len(parts) + [VMEM],
        out_specs=(VMEM, SMEM),
        name="finish",
    )(*parts, score_head.reshape(1, width))
    count = lax.axis_size("dp")
    partner = lax.ppermute(seq_score, "dp", [(d, d ^ (count // 2)) for d in range(count)])
    pair_score = jnp.abs(seq_score - partner) + 0.5 * (seq_score + partner)
    return mixed, pair_score


def solution(mesh):
    tokens, whole = P(("dp", "expert"), None), P()
    weights = P("expert", None, None)
    return jax.shard_map(
        body,
        mesh=mesh,
        in_specs=(tokens, tokens, tokens, P(("dp", "expert")), whole, weights, weights, weights, whole),
        out_specs=(tokens, P(("dp", "expert"))),
        check_vma=False,
    )
```

```python
import functools

import jax
import jax.numpy as jnp
from jax import lax
from jax.experimental import pallas as pl
from jax.experimental.pallas import tpu as pltpu
from jax.sharding import PartitionSpec as P

SEQ_LEN = 16
MOST = 24
META = 128
MIB = 1 << 20

VMEM = pl.BlockSpec(memory_space=pltpu.VMEM)
SMEM = pl.BlockSpec(memory_space=pltpu.SMEM)
HBM = pl.BlockSpec(memory_space=pltpu.HBM)


def prep_kernel(experts, tok_ref, ids_ref, gate_ref, scorer_ref, tags_ref, out_ref):
    rows, width = tok_ref.shape
    for s in range(rows // SEQ_LEN):
        span = pl.ds(s * SEQ_LEN, SEQ_LEN)
        tag = jnp.where(scorer_ref[s] == 1, tags_ref[1:2, :], tags_ref[0:1, :]).astype(jnp.float32)
        out_ref[span, 0:width] = (tok_ref[span, :].astype(jnp.float32) + tag).astype(jnp.bfloat16)
    fixed = gate_ref[...].astype(jnp.float32)
    weight = fixed / jnp.sum(fixed, axis=0, keepdims=True)
    high = weight.astype(jnp.bfloat16).astype(jnp.float32)
    low = weight - high
    ids = ids_ref[...]
    place = lax.broadcasted_iota(jnp.int32, (META, rows), 0)
    meta = jnp.zeros((META, rows), jnp.float32)
    for k in range(ids.shape[0]):
        one = ids[k : k + 1, :]
        meta = meta + jnp.where(place == one, high[k : k + 1, :], 0.0)
        meta = meta + jnp.where(place == one + experts, low[k : k + 1, :], 0.0)
    out_ref[:, width : width + META] = meta.T.astype(jnp.bfloat16)


def pick_rows(meta, first, per_device, experts):
    rows = meta.shape[0]
    room = 2 * MOST
    lane = lax.broadcasted_iota(jnp.int32, meta.shape, 1)
    routed = (meta > 0) & (lane < experts)
    row = lax.broadcasted_iota(jnp.int32, (rows, rows), 0)
    col = lax.broadcasted_iota(jnp.int32, (rows, rows), 1)
    earlier = (row > col).astype(jnp.bfloat16)
    rank = jnp.dot(earlier, routed.astype(jnp.bfloat16), preferred_element_type=jnp.float32)
    rank = jnp.where(routed, rank, -1.0)
    slot = lax.broadcasted_iota(jnp.int32, (rows, per_device * room), 1)
    hit = jnp.zeros((rows, per_device * room), jnp.bool_)
    for e in range(per_device):
        mine = jnp.max(jnp.where(lane == first + e, rank, -1.0), axis=1, keepdims=True).astype(jnp.int32)
        hit = hit | ((mine >= 0) & (slot == mine + e * room))
    return hit.astype(jnp.float32).astype(jnp.bfloat16)


def ffn_kernel(chips, experts, *refs):
    x_refs, (wg, wu, wd), refs = refs[: 2 * chips], refs[2 * chips : 2 * chips + 3], refs[2 * chips + 3 :]
    out_refs, (g_ref, pick_ref, o_ref) = refs[: 2 * chips], refs[2 * chips :]
    per_device, width, ff = wg.shape
    room = 2 * MOST
    first = lax.axis_index("expert") * per_device
    for k in range(chips):
        x = jnp.concatenate([x_refs[2 * k][...], x_refs[2 * k + 1][...]], axis=0)
        pick = pick_rows(x[:, width:].astype(jnp.float32), first, per_device, experts)
        pick_ref[k] = pick
        picked = lax.dot_general(pick, x, (((0,), (0,)), ((), ())), preferred_element_type=jnp.float32)
        picked = picked.astype(jnp.bfloat16)
        for e in range(per_device):
            g_ref[e, k * room : (k + 1) * room, :] = picked[e * room : (e + 1) * room, :]
    lane = lax.broadcasted_iota(jnp.int32, (chips * room, META), 1)
    for e in range(per_device):
        x = g_ref[e, :, 0:width]
        meta = g_ref[e, :, width:].astype(jnp.float32)
        mine = (lane == first + e) | (lane == first + e + experts)
        weight = jnp.sum(jnp.where(mine, meta, 0.0), axis=1, keepdims=True)
        gate = jnp.dot(x, wg[e], preferred_element_type=jnp.float32)
        up = jnp.dot(x, wu[e], preferred_element_type=jnp.float32)
        hidden = (gate / (1.0 + jnp.exp(-gate)) * up * weight).astype(jnp.bfloat16)
        out = jnp.dot(hidden, wd[e], preferred_element_type=jnp.float32).astype(jnp.bfloat16)
        for k in range(chips):
            o_ref[k, e * room : (e + 1) * room, :] = out[k * room : (k + 1) * room, :]
    for k in range(chips):
        rows = jnp.dot(pick_ref[k], o_ref[k], preferred_element_type=jnp.float32).astype(jnp.bfloat16)
        half = rows.shape[0] // 2
        out_refs[2 * k][...] = rows[:half]
        out_refs[2 * k + 1][...] = rows[half:]


def far_memory(x):
    return pltpu.with_memory_space_constraint(x, pltpu.HBM)


def load_kernel(x_ref, *refs):
    count = (len(refs) - 1) // 2
    sems = refs[-1]
    copies = []
    for j in range(count):
        for e in range(refs[j].shape[0]):
            copy = pltpu.make_async_copy(refs[j].at[e], refs[count + j].at[e], sems.at[j, e])
            copy.start()
            copies.append(copy)
    for copy in copies:
        copy.wait()


def load(after, *arrays):
    return pl.pallas_call(
        load_kernel,
        out_shape=[pltpu.VMEM(a.shape, a.dtype) for a in arrays],
        in_specs=[VMEM] + [HBM] * len(arrays),
        out_specs=[VMEM] * len(arrays),
        scratch_shapes=[pltpu.SemaphoreType.DMA((len(arrays), arrays[0].shape[0]))],
        compiler_params=pltpu.CompilerParams(vmem_limit_bytes=MIB),
        cost_estimate=pl.CostEstimate(
            flops=0, bytes_accessed=sum(a.size * a.dtype.itemsize for a in arrays), transcendentals=0
        ),
        name="load_weights",
    )(near_memory(after), *map(far_memory, arrays))


def near_memory(x):
    return pltpu.with_memory_space_constraint(x, pltpu.VMEM)


def ffn(name, sources, experts, weights):
    per_device, width, ff = weights[0].shape
    xs = [near_memory(x) for pair in sources for x in pair]
    rows = xs[0].shape[0]
    chips = len(sources)
    room = 2 * MOST
    outs = pl.pallas_call(
        functools.partial(ffn_kernel, chips, experts),
        out_shape=[pltpu.VMEM((rows, width), jnp.bfloat16)] * (2 * chips),
        in_specs=[VMEM] * (len(xs) + 3),
        out_specs=[VMEM] * (2 * chips),
        scratch_shapes=[
            pltpu.VMEM((per_device, chips * room, width + META), jnp.bfloat16),
            pltpu.VMEM((chips, 2 * rows, per_device * room), jnp.bfloat16),
            pltpu.VMEM((chips, per_device * room, width), jnp.bfloat16),
        ],
        compiler_params=pltpu.CompilerParams(vmem_limit_bytes=16 * MIB),
        cost_estimate=pl.CostEstimate(
            flops=6 * per_device * chips * room * width * ff,
            bytes_accessed=6 * per_device * width * ff,
            transcendentals=0,
        ),
        name=name,
    )(*xs, *map(near_memory, weights))
    return [(outs[2 * k], outs[2 * k + 1]) for k in range(chips)]


def finish_kernel(n_parts, *refs):
    parts, head_ref, mixed_ref, score_ref = refs[:n_parts], *refs[n_parts:]
    rows = mixed_ref.shape[0]
    total = parts[0][...].astype(jnp.float32)
    for part in parts[1:]:
        total = total + part[...].astype(jnp.float32)
    mixed = total.astype(jnp.bfloat16)
    mixed_ref[...] = mixed
    for s, score in enumerate(sequence_scores(mixed, head_ref[...])):
        score_ref[s] = score


def sequence_scores(rows, head):
    scored = rows.astype(jnp.float32) * head
    return [jnp.sum(scored[at : at + SEQ_LEN, :]) for at in range(0, rows.shape[0], SEQ_LEN)]


def on_inner_chip():
    chip = lax.axis_index("expert") // 2
    return (chip == 1) | (chip == 2)


def score_tile(tile, row, rows, head):
    at = lax.broadcasted_iota(jnp.int32, tile.shape, 0)
    lane = lax.broadcasted_iota(jnp.int32, tile.shape, 1)
    for s, score in enumerate(sequence_scores(rows, head)):
        tile = jnp.where((at == row) & (lane == s), score, tile)
    return tile


def own_kernel(own_ref, swapped_ref, near_ref, relayed_ref, head_ref, sum_ref, joins_ref, score_ref):
    relayed = relayed_ref[...]
    inner = on_inner_chip()
    stays = relayed.astype(jnp.float32) * jnp.where(inner, 0.0, 1.0)
    joins_ref[...] = (relayed.astype(jnp.float32) * jnp.where(inner, 1.0, 0.0)).astype(jnp.bfloat16)
    own = own_ref[...].astype(jnp.float32) + swapped_ref[...].astype(jnp.float32) + stays
    sum_ref[...] = own
    head = head_ref[...]
    tile = score_tile(jnp.zeros(score_ref.shape, jnp.float32), 0, near_ref[...], head)
    score_ref[...] = score_tile(tile, 2, own, head)


def third_kernel(same_ref, swapped_ref, joins_ref, score_ref, head_ref, back_ref, out_score_ref):
    back = same_ref[...].astype(jnp.float32) + swapped_ref[...].astype(jnp.float32)
    back = (back + joins_ref[...].astype(jnp.float32)).astype(jnp.bfloat16)
    back_ref[...] = back
    out_score_ref[...] = score_tile(score_ref[...], 1, back, head_ref[...])


def both_kernel(score_ref, partner_ref, both_ref):
    both_ref[0] = score_ref[...]
    both_ref[1] = partner_ref[...]


def last_kernel(sum_ref, near_ref, third_ref, both_ref, from_near_ref, from_third_ref, mixed_ref, pair_ref):
    total = sum_ref[...] + near_ref[...].astype(jnp.float32) + third_ref[...].astype(jnp.float32)
    mixed_ref[...] = total.astype(jnp.bfloat16)
    own, partner = (from_near_ref[i, 0:1] + from_third_ref[i, 1:2] + both_ref[i, 2:3] for i in (0, 1))
    pair = jnp.abs(own - partner) + 0.5 * (own + partner)
    lane = lax.broadcasted_iota(jnp.int32, pair.shape, 1)
    for s in range(pair_ref.shape[0]):
        pair_ref[s] = jnp.sum(jnp.where(lane == s, pair, 0.0))


def local_call(kernel, name, out_shape, *xs, out_specs=None):
    return pl.pallas_call(
        kernel,
        out_shape=out_shape,
        in_specs=[VMEM] * len(xs),
        out_specs=out_specs or [VMEM] * len(out_shape),
        compiler_params=pltpu.CompilerParams(vmem_limit_bytes=16 * MIB),
        name=name,
    )(*map(near_memory, xs))


def send(x, route):
    return lax.ppermute(x, "expert", route)


def body(tokens, expert_ids, gate_fixed, scorer_id, direction_tags, w_gate, w_up, w_down, score_head):
    devices = lax.axis_size("expert")
    chips = devices // 2
    experts = w_gate.shape[0] * devices
    rows, width = tokens.shape
    x = pl.pallas_call(
        functools.partial(prep_kernel, experts),
        out_shape=pltpu.VMEM((rows, width + META), jnp.bfloat16),
        in_specs=[VMEM, VMEM, VMEM, SMEM, VMEM],
        out_specs=VMEM,
        name="prep",
    )(tokens, expert_ids.T, gate_fixed.T, scorer_id, direction_tags)
    weights = load(x, w_gate, w_up, w_down)

    def exchange(block, k):
        return send(block, [(d, d ^ (2 * k)) for d in range(devices)])

    def core_swap(block):
        return send(block, [(d, d ^ 1) for d in range(devices)])

    def pair(block):
        return block, core_swap(block)

    def partner_of(block):
        count = lax.axis_size("dp")
        return lax.ppermute(block, "dp", [(d, d ^ (count // 2)) for d in range(count)])

    def chip_sum(sums):
        same, other = sums
        return (same.astype(jnp.float32) + core_swap(other).astype(jnp.float32)).astype(jnp.bfloat16)

    def chip_route(*pairs):
        return [(2 * a + c, 2 * b + c) for a, b in pairs for c in (0, 1)]

    if chips == 4:
        far = exchange(x, 2)
        near = exchange(x, 1)
        x_pair = pair(x)
        far, near, x_pair, *weights = lax.optimization_barrier((far, near, x_pair, *weights))
        third = send(x_pair[0], chip_route((1, 2), (2, 1))) + send(far, chip_route((1, 0), (2, 3)))
        own_sums, near_sums, far_sums = ffn("experts_1", [x_pair, pair(near), pair(far)], experts, weights)
        far_back = chip_sum(far_sums)
        third_pair, far_back = lax.optimization_barrier((pair(third), far_back))
        relayed = send(far_back, chip_route((1, 3), (2, 0), (0, 1), (3, 2)))
        (third_sums,) = ffn("experts_2", [third_pair], experts, weights)
        near_back = chip_sum(near_sums)
        head = score_head.reshape(1, width)
        scores = (8, META)
        own_sum, joins, score = local_call(
            own_kernel,
            "own_sum",
            [
                pltpu.VMEM((rows, width), jnp.float32),
                pltpu.VMEM((rows, width), jnp.bfloat16),
                pltpu.VMEM(scores, jnp.float32),
            ],
            *(own_sums[0], core_swap(own_sums[1]), near_back, relayed, head),
        )
        third_same, third_other = third_sums
        third_other, joins = lax.optimization_barrier((third_other, joins))
        third_back, score = local_call(
            third_kernel,
            "third_back",
            [pltpu.VMEM((rows, width), jnp.bfloat16), pltpu.VMEM(scores, jnp.float32)],
            *(third_same, core_swap(third_other), joins, score, head),
        )
        near_back, third_back = lax.optimization_barrier((near_back, third_back))
        third = exchange(third_back, 3)
        near = exchange(near_back, 1)
        (both,) = local_call(
            both_kernel, "both_scores", [pltpu.VMEM((2, *scores), jnp.float32)], score, partner_of(score)
        )
        return local_call(
            last_kernel,
            "mixed",
            [
                jax.ShapeDtypeStruct((rows, width), jnp.bfloat16),
                jax.ShapeDtypeStruct((rows // SEQ_LEN,), jnp.float32),
            ],
            own_sum,
            near,
            third,
            both,
            exchange(both, 1),
            exchange(both, 3),
            out_specs=[VMEM, SMEM],
        )
    held = [x] + [exchange(x, k) for k in range(1, chips)]
    sums = ffn("experts", [pair(b) for b in held], experts, weights)
    parts = [chip_sum(sums[0])] + [exchange(chip_sum(sums[k]), k) for k in range(1, chips)]
    mixed, seq_score = pl.pallas_call(
        functools.partial(finish_kernel, len(parts)),
        out_shape=(
            jax.ShapeDtypeStruct((rows, width), jnp.bfloat16),
            jax.ShapeDtypeStruct((rows // SEQ_LEN,), jnp.float32),
        ),
        in_specs=[VMEM] * len(parts) + [VMEM],
        out_specs=(VMEM, SMEM),
        name="finish",
    )(*parts, score_head.reshape(1, width))
    partner = partner_of(seq_score)
    pair_score = jnp.abs(seq_score - partner) + 0.5 * (seq_score + partner)
    return mixed, pair_score


def solution(mesh):
    tokens, whole = P(("dp", "expert"), None), P()
    weights = P("expert", None, None)
    return jax.shard_map(
        body,
        mesh=mesh,
        in_specs=(tokens, tokens, tokens, P(("dp", "expert")), whole, weights, weights, weights, whole),
        out_specs=(tokens, P(("dp", "expert"))),
        check_vma=False,
    )
```

```python
import functools

import jax
import jax.numpy as jnp
from jax import lax
from jax.experimental import pallas as pl
from jax.experimental.pallas import tpu as pltpu
from jax.sharding import PartitionSpec as P

SEQ_LEN = 16
MOST = 24
META = 128
MIB = 1 << 20

VMEM = pl.BlockSpec(memory_space=pltpu.VMEM)
SMEM = pl.BlockSpec(memory_space=pltpu.SMEM)
HBM = pl.BlockSpec(memory_space=pltpu.HBM)


def prep_kernel(experts, tok_ref, ids_ref, gate_ref, scorer_ref, tags_ref, out_ref):
    rows, width = tok_ref.shape
    for s in range(rows // SEQ_LEN):
        span = pl.ds(s * SEQ_LEN, SEQ_LEN)
        tag = jnp.where(scorer_ref[s] == 1, tags_ref[1:2, :], tags_ref[0:1, :]).astype(jnp.float32)
        out_ref[span, 0:width] = (tok_ref[span, :].astype(jnp.float32) + tag).astype(jnp.bfloat16)
    fixed = gate_ref[...].astype(jnp.float32)
    weight = fixed / jnp.sum(fixed, axis=0, keepdims=True)
    high = weight.astype(jnp.bfloat16).astype(jnp.float32)
    low = weight - high
    ids = ids_ref[...]
    place = lax.broadcasted_iota(jnp.int32, (META, rows), 0)
    meta = jnp.zeros((META, rows), jnp.float32)
    for k in range(ids.shape[0]):
        one = ids[k : k + 1, :]
        meta = meta + jnp.where(place == one, high[k : k + 1, :], 0.0)
        meta = meta + jnp.where(place == one + experts, low[k : k + 1, :], 0.0)
    out_ref[:, width : width + META] = meta.T.astype(jnp.bfloat16)


def pick_rows(meta, first, per_device, experts):
    rows = meta.shape[0]
    room = 2 * MOST
    lane = lax.broadcasted_iota(jnp.int32, meta.shape, 1)
    routed = (meta > 0) & (lane < experts)
    row = lax.broadcasted_iota(jnp.int32, (rows, rows), 0)
    col = lax.broadcasted_iota(jnp.int32, (rows, rows), 1)
    earlier = (row > col).astype(jnp.bfloat16)
    rank = jnp.dot(earlier, routed.astype(jnp.bfloat16), preferred_element_type=jnp.float32)
    rank = jnp.where(routed, rank, -1.0)
    slot = lax.broadcasted_iota(jnp.int32, (rows, per_device * room), 1)
    hit = jnp.zeros((rows, per_device * room), jnp.bool_)
    for e in range(per_device):
        mine = jnp.max(jnp.where(lane == first + e, rank, -1.0), axis=1, keepdims=True).astype(jnp.int32)
        hit = hit | ((mine >= 0) & (slot == mine + e * room))
    return hit.astype(jnp.float32).astype(jnp.bfloat16)


def ffn_kernel(chips, experts, *refs):
    x_refs, (wg, wu, wd), refs = refs[: 2 * chips], refs[2 * chips : 2 * chips + 3], refs[2 * chips + 3 :]
    out_refs, (g_ref, pick_ref, o_ref) = refs[: 2 * chips], refs[2 * chips :]
    per_device, width, ff = wg.shape
    room = 2 * MOST
    first = lax.axis_index("expert") * per_device
    for k in range(chips):
        x = jnp.concatenate([x_refs[2 * k][...], x_refs[2 * k + 1][...]], axis=0)
        pick = pick_rows(x[:, width:].astype(jnp.float32), first, per_device, experts)
        pick_ref[k] = pick
        picked = lax.dot_general(pick, x, (((0,), (0,)), ((), ())), preferred_element_type=jnp.float32)
        picked = picked.astype(jnp.bfloat16)
        for e in range(per_device):
            g_ref[e, k * room : (k + 1) * room, :] = picked[e * room : (e + 1) * room, :]
    lane = lax.broadcasted_iota(jnp.int32, (chips * room, META), 1)
    for e in range(per_device):
        x = g_ref[e, :, 0:width]
        meta = g_ref[e, :, width:].astype(jnp.float32)
        mine = (lane == first + e) | (lane == first + e + experts)
        weight = jnp.sum(jnp.where(mine, meta, 0.0), axis=1, keepdims=True)
        gate = jnp.dot(x, wg[e], preferred_element_type=jnp.float32)
        up = jnp.dot(x, wu[e], preferred_element_type=jnp.float32)
        hidden = (gate / (1.0 + jnp.exp(-gate)) * up * weight).astype(jnp.bfloat16)
        out = jnp.dot(hidden, wd[e], preferred_element_type=jnp.float32).astype(jnp.bfloat16)
        for k in range(chips):
            o_ref[k, e * room : (e + 1) * room, :] = out[k * room : (k + 1) * room, :]
    for k in range(chips):
        rows = jnp.dot(pick_ref[k], o_ref[k], preferred_element_type=jnp.float32).astype(jnp.bfloat16)
        half = rows.shape[0] // 2
        out_refs[2 * k][...] = rows[:half]
        out_refs[2 * k + 1][...] = rows[half:]


def far_memory(x):
    return pltpu.with_memory_space_constraint(x, pltpu.HBM)


def load_kernel(x_ref, *refs):
    count = (len(refs) - 1) // 2
    sems = refs[-1]
    copies = []
    for j in range(count):
        for e in range(refs[j].shape[0]):
            copy = pltpu.make_async_copy(refs[j].at[e], refs[count + j].at[e], sems.at[j, e])
            copy.start()
            copies.append(copy)
    for copy in copies:
        copy.wait()


def load(after, *arrays):
    return pl.pallas_call(
        load_kernel,
        out_shape=[pltpu.VMEM(a.shape, a.dtype) for a in arrays],
        in_specs=[VMEM] + [HBM] * len(arrays),
        out_specs=[VMEM] * len(arrays),
        scratch_shapes=[pltpu.SemaphoreType.DMA((len(arrays), arrays[0].shape[0]))],
        compiler_params=pltpu.CompilerParams(vmem_limit_bytes=MIB),
        cost_estimate=pl.CostEstimate(
            flops=0, bytes_accessed=sum(a.size * a.dtype.itemsize for a in arrays), transcendentals=0
        ),
        name="load_weights",
    )(near_memory(after), *map(far_memory, arrays))


def near_memory(x):
    return pltpu.with_memory_space_constraint(x, pltpu.VMEM)


def ffn(name, sources, experts, weights):
    per_device, width, ff = weights[0].shape
    xs = [near_memory(x) for pair in sources for x in pair]
    rows = xs[0].shape[0]
    chips = len(sources)
    room = 2 * MOST
    outs = pl.pallas_call(
        functools.partial(ffn_kernel, chips, experts),
        out_shape=[pltpu.VMEM((rows, width), jnp.bfloat16)] * (2 * chips),
        in_specs=[VMEM] * (len(xs) + 3),
        out_specs=[VMEM] * (2 * chips),
        scratch_shapes=[
            pltpu.VMEM((per_device, chips * room, width + META), jnp.bfloat16),
            pltpu.VMEM((chips, 2 * rows, per_device * room), jnp.bfloat16),
            pltpu.VMEM((chips, per_device * room, width), jnp.bfloat16),
        ],
        compiler_params=pltpu.CompilerParams(vmem_limit_bytes=16 * MIB),
        cost_estimate=pl.CostEstimate(
            flops=6 * per_device * chips * room * width * ff,
            bytes_accessed=6 * per_device * width * ff,
            transcendentals=0,
        ),
        name=name,
    )(*xs, *map(near_memory, weights))
    return [(outs[2 * k], outs[2 * k + 1]) for k in range(chips)]


def finish_kernel(n_parts, *refs):
    parts, head_ref, mixed_ref, score_ref = refs[:n_parts], *refs[n_parts:]
    rows = mixed_ref.shape[0]
    total = parts[0][...].astype(jnp.float32)
    for part in parts[1:]:
        total = total + part[...].astype(jnp.float32)
    mixed = total.astype(jnp.bfloat16)
    mixed_ref[...] = mixed
    for s, score in enumerate(sequence_scores(mixed, head_ref[...])):
        score_ref[s] = score


def sequence_scores(rows, head):
    scored = rows.astype(jnp.float32) * head
    return [jnp.sum(scored[at : at + SEQ_LEN, :]) for at in range(0, rows.shape[0], SEQ_LEN)]


def on_inner_chip():
    chip = lax.axis_index("expert") // 2
    return (chip == 1) | (chip == 2)


def score_tile(tile, row, rows, head):
    at = lax.broadcasted_iota(jnp.int32, tile.shape, 0)
    lane = lax.broadcasted_iota(jnp.int32, tile.shape, 1)
    for s, score in enumerate(sequence_scores(rows, head)):
        tile = jnp.where((at == row) & (lane == s), score, tile)
    return tile


def own_kernel(own_ref, swapped_ref, near_ref, relayed_ref, head_ref, sum_ref, joins_ref, score_ref):
    relayed = relayed_ref[...]
    inner = on_inner_chip()
    stays = relayed.astype(jnp.float32) * jnp.where(inner, 0.0, 1.0)
    joins_ref[...] = (relayed.astype(jnp.float32) * jnp.where(inner, 1.0, 0.0)).astype(jnp.bfloat16)
    own = own_ref[...].astype(jnp.float32) + swapped_ref[...].astype(jnp.float32) + stays
    sum_ref[...] = own
    head = head_ref[...]
    tile = score_tile(jnp.zeros(score_ref.shape, jnp.float32), 0, near_ref[...], head)
    score_ref[...] = score_tile(tile, 2, own, head)


def third_kernel(same_ref, swapped_ref, joins_ref, score_ref, head_ref, back_ref, out_score_ref):
    back = same_ref[...].astype(jnp.float32) + swapped_ref[...].astype(jnp.float32)
    back = (back + joins_ref[...].astype(jnp.float32)).astype(jnp.bfloat16)
    back_ref[...] = back
    out_score_ref[...] = score_tile(score_ref[...], 1, back, head_ref[...])


def both_kernel(score_ref, partner_ref, both_ref):
    both_ref[0] = score_ref[...]
    both_ref[1] = partner_ref[...]


def last_kernel(sum_ref, near_ref, third_ref, both_ref, from_near_ref, from_third_ref, mixed_ref, pair_ref):
    total = sum_ref[...] + near_ref[...].astype(jnp.float32) + third_ref[...].astype(jnp.float32)
    mixed_ref[...] = total.astype(jnp.bfloat16)
    own, partner = (from_near_ref[i, 0:1] + from_third_ref[i, 1:2] + both_ref[i, 2:3] for i in (0, 1))
    pair = jnp.abs(own - partner) + 0.5 * (own + partner)
    lane = lax.broadcasted_iota(jnp.int32, pair.shape, 1)
    for s in range(pair_ref.shape[0]):
        pair_ref[s] = jnp.sum(jnp.where(lane == s, pair, 0.0))


def local_call(kernel, name, out_shape, *xs, out_specs=None):
    return pl.pallas_call(
        kernel,
        out_shape=out_shape,
        in_specs=[VMEM] * len(xs),
        out_specs=out_specs or [VMEM] * len(out_shape),
        compiler_params=pltpu.CompilerParams(vmem_limit_bytes=16 * MIB),
        name=name,
    )(*map(near_memory, xs))


def send(x, route):
    return lax.ppermute(x, "expert", route)


def body(tokens, expert_ids, gate_fixed, scorer_id, direction_tags, w_gate, w_up, w_down, score_head):
    devices = lax.axis_size("expert")
    chips = devices // 2
    experts = w_gate.shape[0] * devices
    rows, width = tokens.shape
    x = pl.pallas_call(
        functools.partial(prep_kernel, experts),
        out_shape=pltpu.VMEM((rows, width + META), jnp.bfloat16),
        in_specs=[VMEM, VMEM, VMEM, SMEM, VMEM],
        out_specs=VMEM,
        name="prep",
    )(tokens, expert_ids.T, gate_fixed.T, scorer_id, direction_tags)
    weights = load(x, w_gate, w_up, w_down)

    def exchange(block, k):
        return send(block, [(d, d ^ (2 * k)) for d in range(devices)])

    def core_swap(block):
        return send(block, [(d, d ^ 1) for d in range(devices)])

    def pair(block):
        return block, core_swap(block)

    def partner_of(block):
        count = lax.axis_size("dp")
        return lax.ppermute(block, "dp", [(d, d ^ (count // 2)) for d in range(count)])

    def chip_sum(sums):
        same, other = sums
        return (same.astype(jnp.float32) + core_swap(other).astype(jnp.float32)).astype(jnp.bfloat16)

    def chip_route(*pairs):
        return [(2 * a + c, 2 * b + c) for a, b in pairs for c in (0, 1)]

    if chips == 4:
        far = exchange(x, 2)
        near = exchange(x, 1)
        x_pair = pair(x)
        far, near, x_pair, *weights = lax.optimization_barrier((far, near, x_pair, *weights))
        third = exchange(far, 1)
        own_sums, near_sums, far_sums = ffn("experts_1", [x_pair, pair(near), pair(far)], experts, weights)
        far_back = chip_sum(far_sums)
        relayed = send(far_back, chip_route((1, 3), (2, 0), (0, 1), (3, 2)))
        (third_sums,) = ffn("experts_2", [pair(third)], experts, weights)
        third_same, third_other = third_sums
        near_back = chip_sum(near_sums)
        third_other, near_back, relayed = lax.optimization_barrier((third_other, near_back, relayed))
        near = exchange(near_back, 1)
        head = score_head.reshape(1, width)
        scores = (8, META)
        own_sum, joins, score = local_call(
            own_kernel,
            "own_sum",
            [
                pltpu.VMEM((rows, width), jnp.float32),
                pltpu.VMEM((rows, width), jnp.bfloat16),
                pltpu.VMEM(scores, jnp.float32),
            ],
            *(own_sums[0], core_swap(own_sums[1]), near_back, relayed, head),
        )
        third_back, score = local_call(
            third_kernel,
            "third_back",
            [pltpu.VMEM((rows, width), jnp.bfloat16), pltpu.VMEM(scores, jnp.float32)],
            *(third_same, core_swap(third_other), joins, score, head),
        )
        third = exchange(third_back, 3)
        (both,) = local_call(
            both_kernel, "both_scores", [pltpu.VMEM((2, *scores), jnp.float32)], score, partner_of(score)
        )
        return local_call(
            last_kernel,
            "mixed",
            [
                jax.ShapeDtypeStruct((rows, width), jnp.bfloat16),
                jax.ShapeDtypeStruct((rows // SEQ_LEN,), jnp.float32),
            ],
            own_sum,
            near,
            third,
            both,
            exchange(both, 1),
            exchange(both, 3),
            out_specs=[VMEM, SMEM],
        )
    held = [x] + [exchange(x, k) for k in range(1, chips)]
    sums = ffn("experts", [pair(b) for b in held], experts, weights)
    parts = [chip_sum(sums[0])] + [exchange(chip_sum(sums[k]), k) for k in range(1, chips)]
    mixed, seq_score = pl.pallas_call(
        functools.partial(finish_kernel, len(parts)),
        out_shape=(
            jax.ShapeDtypeStruct((rows, width), jnp.bfloat16),
            jax.ShapeDtypeStruct((rows // SEQ_LEN,), jnp.float32),
        ),
        in_specs=[VMEM] * len(parts) + [VMEM],
        out_specs=(VMEM, SMEM),
        name="finish",
    )(*parts, score_head.reshape(1, width))
    partner = partner_of(seq_score)
    pair_score = jnp.abs(seq_score - partner) + 0.5 * (seq_score + partner)
    return mixed, pair_score


def solution(mesh):
    tokens, whole = P(("dp", "expert"), None), P()
    weights = P("expert", None, None)
    return jax.shard_map(
        body,
        mesh=mesh,
        in_specs=(tokens, tokens, tokens, P(("dp", "expert")), whole, weights, weights, weights, whole),
        out_specs=(tokens, P(("dp", "expert"))),
        check_vma=False,
    )
```

```python
import functools

import jax
import jax.numpy as jnp
from jax import lax
from jax.experimental import pallas as pl
from jax.experimental.pallas import tpu as pltpu
from jax.sharding import PartitionSpec as P

SEQ_LEN = 16
MOST = 24
META = 128
MIB = 1 << 20

VMEM = pl.BlockSpec(memory_space=pltpu.VMEM)
SMEM = pl.BlockSpec(memory_space=pltpu.SMEM)
HBM = pl.BlockSpec(memory_space=pltpu.HBM)


def prep_kernel(experts, tok_ref, ids_ref, gate_ref, scorer_ref, tags_ref, out_ref):
    rows, width = tok_ref.shape
    for s in range(rows // SEQ_LEN):
        span = pl.ds(s * SEQ_LEN, SEQ_LEN)
        tag = jnp.where(scorer_ref[s] == 1, tags_ref[1:2, :], tags_ref[0:1, :]).astype(jnp.float32)
        out_ref[span, 0:width] = (tok_ref[span, :].astype(jnp.float32) + tag).astype(jnp.bfloat16)
    fixed = gate_ref[...].astype(jnp.float32)
    weight = fixed / jnp.sum(fixed, axis=0, keepdims=True)
    high = weight.astype(jnp.bfloat16).astype(jnp.float32)
    low = weight - high
    ids = ids_ref[...]
    place = lax.broadcasted_iota(jnp.int32, (META, rows), 0)
    meta = jnp.zeros((META, rows), jnp.float32)
    for k in range(ids.shape[0]):
        one = ids[k : k + 1, :]
        meta = meta + jnp.where(place == one, high[k : k + 1, :], 0.0)
        meta = meta + jnp.where(place == one + experts, low[k : k + 1, :], 0.0)
    out_ref[:, width : width + META] = meta.T.astype(jnp.bfloat16)


def pick_rows(meta, first, per_device, experts):
    rows = meta.shape[0]
    room = 2 * MOST
    lane = lax.broadcasted_iota(jnp.int32, meta.shape, 1)
    routed = (meta > 0) & (lane < experts)
    row = lax.broadcasted_iota(jnp.int32, (rows, rows), 0)
    col = lax.broadcasted_iota(jnp.int32, (rows, rows), 1)
    earlier = (row > col).astype(jnp.bfloat16)
    rank = jnp.dot(earlier, routed.astype(jnp.bfloat16), preferred_element_type=jnp.float32)
    rank = jnp.where(routed, rank, -1.0)
    slot = lax.broadcasted_iota(jnp.int32, (rows, per_device * room), 1)
    hit = jnp.zeros((rows, per_device * room), jnp.bool_)
    for e in range(per_device):
        mine = jnp.max(jnp.where(lane == first + e, rank, -1.0), axis=1, keepdims=True).astype(jnp.int32)
        hit = hit | ((mine >= 0) & (slot == mine + e * room))
    return hit.astype(jnp.float32).astype(jnp.bfloat16)


def ffn_kernel(chips, experts, *refs):
    x_refs, (wg, wu, wd), refs = refs[: 2 * chips], refs[2 * chips : 2 * chips + 3], refs[2 * chips + 3 :]
    out_refs, (g_ref, pick_ref, o_ref) = refs[: 2 * chips], refs[2 * chips :]
    per_device, width, ff = wg.shape
    room = 2 * MOST
    first = lax.axis_index("expert") * per_device
    for k in range(chips):
        x = jnp.concatenate([x_refs[2 * k][...], x_refs[2 * k + 1][...]], axis=0)
        pick = pick_rows(x[:, width:].astype(jnp.float32), first, per_device, experts)
        pick_ref[k] = pick
        picked = lax.dot_general(pick, x, (((0,), (0,)), ((), ())), preferred_element_type=jnp.float32)
        picked = picked.astype(jnp.bfloat16)
        for e in range(per_device):
            g_ref[e, k * room : (k + 1) * room, :] = picked[e * room : (e + 1) * room, :]
    lane = lax.broadcasted_iota(jnp.int32, (chips * room, META), 1)
    for e in range(per_device):
        x = g_ref[e, :, 0:width]
        meta = g_ref[e, :, width:].astype(jnp.float32)
        mine = (lane == first + e) | (lane == first + e + experts)
        weight = jnp.sum(jnp.where(mine, meta, 0.0), axis=1, keepdims=True)
        gate = jnp.dot(x, wg[e], preferred_element_type=jnp.float32)
        up = jnp.dot(x, wu[e], preferred_element_type=jnp.float32)
        hidden = (gate / (1.0 + jnp.exp(-gate)) * up * weight).astype(jnp.bfloat16)
        out = jnp.dot(hidden, wd[e], preferred_element_type=jnp.float32).astype(jnp.bfloat16)
        for k in range(chips):
            o_ref[k, e * room : (e + 1) * room, :] = out[k * room : (k + 1) * room, :]
    for k in range(chips):
        rows = jnp.dot(pick_ref[k], o_ref[k], preferred_element_type=jnp.float32).astype(jnp.bfloat16)
        half = rows.shape[0] // 2
        out_refs[2 * k][...] = rows[:half]
        out_refs[2 * k + 1][...] = rows[half:]


def far_memory(x):
    return pltpu.with_memory_space_constraint(x, pltpu.HBM)


def load_kernel(x_ref, *refs):
    count = (len(refs) - 1) // 2
    sems = refs[-1]
    copies = []
    for j in range(count):
        for e in range(refs[j].shape[0]):
            copy = pltpu.make_async_copy(refs[j].at[e], refs[count + j].at[e], sems.at[j, e])
            copy.start()
            copies.append(copy)
    for copy in copies:
        copy.wait()


def load(after, *arrays):
    return pl.pallas_call(
        load_kernel,
        out_shape=[pltpu.VMEM(a.shape, a.dtype) for a in arrays],
        in_specs=[VMEM] + [HBM] * len(arrays),
        out_specs=[VMEM] * len(arrays),
        scratch_shapes=[pltpu.SemaphoreType.DMA((len(arrays), arrays[0].shape[0]))],
        compiler_params=pltpu.CompilerParams(vmem_limit_bytes=MIB),
        cost_estimate=pl.CostEstimate(
            flops=0, bytes_accessed=sum(a.size * a.dtype.itemsize for a in arrays), transcendentals=0
        ),
        name="load_weights",
    )(near_memory(after), *map(far_memory, arrays))


def near_memory(x):
    return pltpu.with_memory_space_constraint(x, pltpu.VMEM)


def ffn(name, sources, experts, weights):
    per_device, width, ff = weights[0].shape
    xs = [near_memory(x) for pair in sources for x in pair]
    rows = xs[0].shape[0]
    chips = len(sources)
    room = 2 * MOST
    outs = pl.pallas_call(
        functools.partial(ffn_kernel, chips, experts),
        out_shape=[pltpu.VMEM((rows, width), jnp.bfloat16)] * (2 * chips),
        in_specs=[VMEM] * (len(xs) + 3),
        out_specs=[VMEM] * (2 * chips),
        scratch_shapes=[
            pltpu.VMEM((per_device, chips * room, width + META), jnp.bfloat16),
            pltpu.VMEM((chips, 2 * rows, per_device * room), jnp.bfloat16),
            pltpu.VMEM((chips, per_device * room, width), jnp.bfloat16),
        ],
        compiler_params=pltpu.CompilerParams(vmem_limit_bytes=16 * MIB),
        cost_estimate=pl.CostEstimate(
            flops=6 * per_device * chips * room * width * ff,
            bytes_accessed=6 * per_device * width * ff,
            transcendentals=0,
        ),
        name=name,
    )(*xs, *map(near_memory, weights))
    return [(outs[2 * k], outs[2 * k + 1]) for k in range(chips)]


def finish_kernel(n_parts, *refs):
    parts, head_ref, mixed_ref, score_ref = refs[:n_parts], *refs[n_parts:]
    rows = mixed_ref.shape[0]
    total = parts[0][...].astype(jnp.float32)
    for part in parts[1:]:
        total = total + part[...].astype(jnp.float32)
    mixed = total.astype(jnp.bfloat16)
    mixed_ref[...] = mixed
    for s, score in enumerate(sequence_scores(mixed, head_ref[...])):
        score_ref[s] = score


def sequence_scores(rows, head):
    scored = rows.astype(jnp.float32) * head
    return [jnp.sum(scored[at : at + SEQ_LEN, :]) for at in range(0, rows.shape[0], SEQ_LEN)]


def on_inner_chip():
    chip = lax.axis_index("expert") // 2
    return (chip == 1) | (chip == 2)


def score_tile(tile, row, rows, head):
    at = lax.broadcasted_iota(jnp.int32, tile.shape, 0)
    lane = lax.broadcasted_iota(jnp.int32, tile.shape, 1)
    for s, score in enumerate(sequence_scores(rows, head)):
        tile = jnp.where((at == row) & (lane == s), score, tile)
    return tile


def third_kernel(sum_ref, relayed_ref, back_ref):
    joins = relayed_ref[...].astype(jnp.float32) * jnp.where(on_inner_chip(), 1.0, 0.0)
    back_ref[...] = (sum_ref[...] + joins).astype(jnp.bfloat16)


def own_kernel(own_ref, swapped_ref, relayed_ref, near_ref, third_ref, head_ref, sum_ref, score_ref):
    stays = relayed_ref[...].astype(jnp.float32) * jnp.where(on_inner_chip(), 0.0, 1.0)
    own = own_ref[...].astype(jnp.float32) + swapped_ref[...].astype(jnp.float32) + stays
    sum_ref[...] = own
    head = head_ref[...]
    tile = jnp.zeros(score_ref.shape, jnp.float32)
    for row, value in enumerate((near_ref[...], third_ref[...], own)):
        tile = score_tile(tile, row, value, head)
    score_ref[...] = tile


def both_kernel(score_ref, partner_ref, both_ref):
    both_ref[0] = score_ref[...]
    both_ref[1] = partner_ref[...]


def last_kernel(sum_ref, near_ref, third_ref, both_ref, from_near_ref, from_third_ref, mixed_ref, pair_ref):
    total = sum_ref[...] + near_ref[...].astype(jnp.float32) + third_ref[...].astype(jnp.float32)
    mixed_ref[...] = total.astype(jnp.bfloat16)
    own, partner = (from_near_ref[i, 0:1] + from_third_ref[i, 1:2] + both_ref[i, 2:3] for i in (0, 1))
    pair = jnp.abs(own - partner) + 0.5 * (own + partner)
    lane = lax.broadcasted_iota(jnp.int32, pair.shape, 1)
    for s in range(pair_ref.shape[0]):
        pair_ref[s] = jnp.sum(jnp.where(lane == s, pair, 0.0))


def local_call(kernel, name, out_shape, *xs, out_specs=None):
    return pl.pallas_call(
        kernel,
        out_shape=out_shape,
        in_specs=[VMEM] * len(xs),
        out_specs=out_specs or [VMEM] * len(out_shape),
        compiler_params=pltpu.CompilerParams(vmem_limit_bytes=16 * MIB),
        name=name,
    )(*map(near_memory, xs))


def send(x, route):
    return lax.ppermute(x, "expert", route)


def body(tokens, expert_ids, gate_fixed, scorer_id, direction_tags, w_gate, w_up, w_down, score_head):
    devices = lax.axis_size("expert")
    chips = devices // 2
    experts = w_gate.shape[0] * devices
    rows, width = tokens.shape
    x = pl.pallas_call(
        functools.partial(prep_kernel, experts),
        out_shape=pltpu.VMEM((rows, width + META), jnp.bfloat16),
        in_specs=[VMEM, VMEM, VMEM, SMEM, VMEM],
        out_specs=VMEM,
        name="prep",
    )(tokens, expert_ids.T, gate_fixed.T, scorer_id, direction_tags)
    weights = load(x, w_gate, w_up, w_down)

    def exchange(block, k):
        return send(block, [(d, d ^ (2 * k)) for d in range(devices)])

    def core_swap(block):
        return send(block, [(d, d ^ 1) for d in range(devices)])

    def pair(block):
        return block, core_swap(block)

    def partner_of(block):
        count = lax.axis_size("dp")
        return lax.ppermute(block, "dp", [(d, d ^ (count // 2)) for d in range(count)])

    def chip_sum(sums, dtype=jnp.bfloat16):
        same, other = sums
        return (same.astype(jnp.float32) + core_swap(other).astype(jnp.float32)).astype(dtype)

    def chip_route(*pairs):
        return [(2 * a + c, 2 * b + c) for a, b in pairs for c in (0, 1)]

    if chips == 4:
        far = exchange(x, 2)
        near = exchange(x, 1)
        near, far, x, *weights = lax.optimization_barrier((near, far, x, *weights))
        third = exchange(far, 1)
        far_sums, near_sums = ffn("experts_far_near", [pair(far), pair(near)], experts, weights)
        far_back = chip_sum(far_sums)
        relayed = send(far_back, chip_route((1, 3), (2, 0), (0, 1), (3, 2)))
        third_sums, own_sums = ffn("experts_third_own", [pair(third), pair(x)], experts, weights)
        near_back = chip_sum(near_sums)
        third_same, near_back = lax.optimization_barrier((third_sums[0], near_back))
        near = exchange(near_back, 1)
        (third_back,) = local_call(
            third_kernel, "third_back", [pltpu.VMEM((rows, width), jnp.bfloat16)], chip_sum((third_same, third_sums[1]), jnp.float32), relayed
        )
        third = exchange(third_back, 3)
        scores = (8, META)
        own_sum, score = local_call(
            own_kernel,
            "own_sum",
            [pltpu.VMEM((rows, width), jnp.float32), pltpu.VMEM(scores, jnp.float32)],
            *(own_sums[0], core_swap(own_sums[1]), relayed, near_back, third_back, score_head.reshape(1, width)),
        )
        (both,) = local_call(
            both_kernel, "both_scores", [pltpu.VMEM((2, *scores), jnp.float32)], score, partner_of(score)
        )
        return local_call(
            last_kernel,
            "mixed",
            [
                jax.ShapeDtypeStruct((rows, width), jnp.bfloat16),
                jax.ShapeDtypeStruct((rows // SEQ_LEN,), jnp.float32),
            ],
            own_sum,
            near,
            third,
            both,
            exchange(both, 1),
            exchange(both, 3),
            out_specs=[VMEM, SMEM],
        )
    held = [x] + [exchange(x, k) for k in range(1, chips)]
    sums = ffn("experts", [pair(b) for b in held], experts, weights)
    parts = [chip_sum(sums[0])] + [exchange(chip_sum(sums[k]), k) for k in range(1, chips)]
    mixed, seq_score = pl.pallas_call(
        functools.partial(finish_kernel, len(parts)),
        out_shape=(
            jax.ShapeDtypeStruct((rows, width), jnp.bfloat16),
            jax.ShapeDtypeStruct((rows // SEQ_LEN,), jnp.float32),
        ),
        in_specs=[VMEM] * len(parts) + [VMEM],
        out_specs=(VMEM, SMEM),
        name="finish",
    )(*parts, score_head.reshape(1, width))
    partner = partner_of(seq_score)
    pair_score = jnp.abs(seq_score - partner) + 0.5 * (seq_score + partner)
    return mixed, pair_score


def solution(mesh):
    tokens, whole = P(("dp", "expert"), None), P()
    weights = P("expert", None, None)
    return jax.shard_map(
        body,
        mesh=mesh,
        in_specs=(tokens, tokens, tokens, P(("dp", "expert")), whole, weights, weights, weights, whole),
        out_specs=(tokens, P(("dp", "expert"))),
        check_vma=False,
    )
```

```python
import functools

import jax
import jax.numpy as jnp
from jax import lax
from jax.experimental import pallas as pl
from jax.experimental.pallas import tpu as pltpu
from jax.sharding import PartitionSpec as P

SEQ_LEN = 16
MOST = 24
META = 128
MIB = 1 << 20

VMEM = pl.BlockSpec(memory_space=pltpu.VMEM)
SMEM = pl.BlockSpec(memory_space=pltpu.SMEM)
HBM = pl.BlockSpec(memory_space=pltpu.HBM)


def prep_kernel(experts, tok_ref, ids_ref, gate_ref, scorer_ref, tags_ref, out_ref):
    rows, width = tok_ref.shape
    for s in range(rows // SEQ_LEN):
        span = pl.ds(s * SEQ_LEN, SEQ_LEN)
        tag = jnp.where(scorer_ref[s] == 1, tags_ref[1:2, :], tags_ref[0:1, :]).astype(jnp.float32)
        out_ref[span, 0:width] = (tok_ref[span, :].astype(jnp.float32) + tag).astype(jnp.bfloat16)
    fixed = gate_ref[...].astype(jnp.float32)
    weight = fixed / jnp.sum(fixed, axis=0, keepdims=True)
    high = weight.astype(jnp.bfloat16).astype(jnp.float32)
    low = weight - high
    ids = ids_ref[...]
    place = lax.broadcasted_iota(jnp.int32, (META, rows), 0)
    meta = jnp.zeros((META, rows), jnp.float32)
    for k in range(ids.shape[0]):
        one = ids[k : k + 1, :]
        meta = meta + jnp.where(place == one, high[k : k + 1, :], 0.0)
        meta = meta + jnp.where(place == one + experts, low[k : k + 1, :], 0.0)
    out_ref[:, width : width + META] = meta.T.astype(jnp.bfloat16)


def pick_rows(meta, first, per_device, experts):
    rows = meta.shape[0]
    room = 2 * MOST
    lane = lax.broadcasted_iota(jnp.int32, meta.shape, 1)
    routed = (meta > 0) & (lane < experts)
    row = lax.broadcasted_iota(jnp.int32, (rows, rows), 0)
    col = lax.broadcasted_iota(jnp.int32, (rows, rows), 1)
    earlier = (row > col).astype(jnp.bfloat16)
    rank = jnp.dot(earlier, routed.astype(jnp.bfloat16), preferred_element_type=jnp.float32)
    rank = jnp.where(routed, rank, -1.0)
    slot = lax.broadcasted_iota(jnp.int32, (rows, per_device * room), 1)
    hit = jnp.zeros((rows, per_device * room), jnp.bool_)
    for e in range(per_device):
        mine = jnp.max(jnp.where(lane == first + e, rank, -1.0), axis=1, keepdims=True).astype(jnp.int32)
        hit = hit | ((mine >= 0) & (slot == mine + e * room))
    return hit.astype(jnp.float32).astype(jnp.bfloat16)


def hidden_rows(x, weight, w_gate, w_up):
    gate = jnp.dot(x, w_gate, preferred_element_type=jnp.float32)
    up = jnp.dot(x, w_up, preferred_element_type=jnp.float32)
    return (gate / (1.0 + jnp.exp(-gate)) * up * weight).astype(jnp.bfloat16)


def expert_weight(meta, expert, experts):
    lane = lax.broadcasted_iota(jnp.int32, meta.shape, 1)
    mine = (lane == expert) | (lane == expert + experts)
    return jnp.sum(jnp.where(mine, meta, 0.0), axis=1, keepdims=True)


def all_rows_kernel(experts, *refs):
    x_refs, (wg, wu, wd), out_refs, (x_ref,) = refs[:2], refs[2:5], refs[5:7], refs[7:]
    per_device, width, ff = wg.shape
    rows = x_refs[0].shape[0]
    first = lax.axis_index("expert") * per_device
    for i, ref in enumerate(x_refs):
        x_ref[i * rows : (i + 1) * rows, :] = ref[...]
    meta = x_ref[:, width:].astype(jnp.float32)

    def hidden_of(e):
        return hidden_rows(x_ref[:, 0:width], expert_weight(meta, first + e, experts), wg[e], wu[e])

    out = 0.0
    hidden = hidden_of(0)
    for e in range(1, per_device):
        following = hidden_of(e)
        out = out + jnp.dot(hidden, wd[e - 1], preferred_element_type=jnp.float32)
        hidden = following
    out = out + jnp.dot(hidden, wd[per_device - 1], preferred_element_type=jnp.float32)
    for i, ref in enumerate(out_refs):
        ref[...] = out[i * rows : (i + 1) * rows].astype(jnp.bfloat16)


def picked_rows_kernel(chips, experts, *refs):
    x_refs, (wg, wu, wd), refs = refs[: 2 * chips], refs[2 * chips : 2 * chips + 3], refs[2 * chips + 3 :]
    out_refs, (g_ref, pick_ref, o_ref) = refs[: 2 * chips], refs[2 * chips :]
    per_device, width, ff = wg.shape
    room = 2 * MOST
    first = lax.axis_index("expert") * per_device
    if g_ref.shape[1] > chips * room:
        g_ref[:, chips * room :, :] = jnp.zeros_like(g_ref[:, chips * room :, :])
    for k in range(chips):
        x = jnp.concatenate([x_refs[2 * k][...], x_refs[2 * k + 1][...]], axis=0)
        pick = pick_rows(x[:, width:].astype(jnp.float32), first, per_device, experts)
        pick_ref[k] = pick
        picked = lax.dot_general(pick, x, (((0,), (0,)), ((), ())), preferred_element_type=jnp.float32)
        picked = picked.astype(jnp.bfloat16)
        for e in range(per_device):
            g_ref[e, k * room : (k + 1) * room, :] = picked[e * room : (e + 1) * room, :]

    def hidden_of(e):
        meta = g_ref[e, :, width:].astype(jnp.float32)
        return hidden_rows(g_ref[e, :, 0:width], expert_weight(meta, first + e, experts), wg[e], wu[e])

    def leave(e, hidden):
        out = jnp.dot(hidden, wd[e], preferred_element_type=jnp.float32).astype(jnp.bfloat16)
        for k in range(chips):
            o_ref[k, e * room : (e + 1) * room, :] = out[k * room : (k + 1) * room, :]

    hidden = hidden_of(0)
    for e in range(1, per_device):
        following = hidden_of(e)
        leave(e - 1, hidden)
        hidden = following
    leave(per_device - 1, hidden)
    for k in range(chips):
        rows = jnp.dot(pick_ref[k], o_ref[k], preferred_element_type=jnp.float32).astype(jnp.bfloat16)
        half = rows.shape[0] // 2
        out_refs[2 * k][...] = rows[:half]
        out_refs[2 * k + 1][...] = rows[half:]


def far_memory(x):
    return pltpu.with_memory_space_constraint(x, pltpu.HBM)


def load_kernel(x_ref, *refs):
    count = (len(refs) - 1) // 2
    sems = refs[-1]
    copies = []
    for j in range(count):
        for e in range(refs[j].shape[0]):
            copy = pltpu.make_async_copy(refs[j].at[e], refs[count + j].at[e], sems.at[j, e])
            copy.start()
            copies.append(copy)
    for copy in copies:
        copy.wait()


def load(after, *arrays):
    return pl.pallas_call(
        load_kernel,
        out_shape=[pltpu.VMEM(a.shape, a.dtype) for a in arrays],
        in_specs=[VMEM] + [HBM] * len(arrays),
        out_specs=[VMEM] * len(arrays),
        scratch_shapes=[pltpu.SemaphoreType.DMA((len(arrays), arrays[0].shape[0]))],
        compiler_params=pltpu.CompilerParams(vmem_limit_bytes=MIB),
        cost_estimate=pl.CostEstimate(
            flops=0, bytes_accessed=sum(a.size * a.dtype.itemsize for a in arrays), transcendentals=0
        ),
        name="load_weights",
    )(near_memory(after), *map(far_memory, arrays))


def near_memory(x):
    return pltpu.with_memory_space_constraint(x, pltpu.VMEM)


def ffn(name, sources, experts, weights):
    per_device, width, ff = weights[0].shape
    xs = [near_memory(x) for pair in sources for x in pair]
    rows = xs[0].shape[0]
    chips = len(sources)
    room = 2 * MOST
    if chips == 1:
        met = 2 * rows
        kernel = functools.partial(all_rows_kernel, experts)
        scratch = [pltpu.VMEM((met, width + META), jnp.bfloat16)]
    else:
        met = -(-chips * room // META) * META
        kernel = functools.partial(picked_rows_kernel, chips, experts)
        scratch = [
            pltpu.VMEM((per_device, met, width + META), jnp.bfloat16),
            pltpu.VMEM((chips, 2 * rows, per_device * room), jnp.bfloat16),
            pltpu.VMEM((chips, per_device * room, width), jnp.bfloat16),
        ]
    outs = pl.pallas_call(
        kernel,
        out_shape=[pltpu.VMEM((rows, width), jnp.bfloat16)] * (2 * chips),
        in_specs=[VMEM] * (len(xs) + 3),
        out_specs=[VMEM] * (2 * chips),
        scratch_shapes=scratch,
        compiler_params=pltpu.CompilerParams(vmem_limit_bytes=16 * MIB),
        cost_estimate=pl.CostEstimate(
            flops=6 * per_device * met * width * ff,
            bytes_accessed=6 * per_device * width * ff,
            transcendentals=0,
        ),
        name=name,
    )(*xs, *map(near_memory, weights))
    return [(outs[2 * k], outs[2 * k + 1]) for k in range(chips)]


def finish_kernel(n_parts, *refs):
    parts, head_ref, mixed_ref, score_ref = refs[:n_parts], *refs[n_parts:]
    rows = mixed_ref.shape[0]
    total = parts[0][...].astype(jnp.float32)
    for part in parts[1:]:
        total = total + part[...].astype(jnp.float32)
    mixed = total.astype(jnp.bfloat16)
    mixed_ref[...] = mixed
    for s, score in enumerate(sequence_scores(mixed, head_ref[...])):
        score_ref[s] = score


def sequence_scores(rows, head):
    scored = rows.astype(jnp.float32) * head
    return [jnp.sum(scored[at : at + SEQ_LEN, :]) for at in range(0, rows.shape[0], SEQ_LEN)]


def on_inner_chip():
    chip = lax.axis_index("expert") // 2
    return (chip == 1) | (chip == 2)


def score_tile(tile, row, rows, head):
    at = lax.broadcasted_iota(jnp.int32, tile.shape, 0)
    lane = lax.broadcasted_iota(jnp.int32, tile.shape, 1)
    for s, score in enumerate(sequence_scores(rows, head)):
        tile = jnp.where((at == row) & (lane == s), score, tile)
    return tile


def third_kernel(sum_ref, relayed_ref, back_ref):
    joins = relayed_ref[...].astype(jnp.float32) * jnp.where(on_inner_chip(), 1.0, 0.0)
    back_ref[...] = (sum_ref[...] + joins).astype(jnp.bfloat16)


def own_kernel(own_ref, swapped_ref, relayed_ref, near_ref, third_ref, head_ref, sum_ref, score_ref):
    stays = relayed_ref[...].astype(jnp.float32) * jnp.where(on_inner_chip(), 0.0, 1.0)
    own = own_ref[...].astype(jnp.float32) + swapped_ref[...].astype(jnp.float32) + stays
    sum_ref[...] = own
    head = head_ref[...]
    tile = jnp.zeros(score_ref.shape, jnp.float32)
    for row, value in enumerate((near_ref[...], third_ref[...], own)):
        tile = score_tile(tile, row, value, head)
    score_ref[...] = tile


def both_kernel(score_ref, partner_ref, both_ref):
    both_ref[0] = score_ref[...]
    both_ref[1] = partner_ref[...]


def last_kernel(sum_ref, near_ref, third_ref, both_ref, from_near_ref, from_third_ref, mixed_ref, pair_ref):
    total = sum_ref[...] + near_ref[...].astype(jnp.float32) + third_ref[...].astype(jnp.float32)
    mixed_ref[...] = total.astype(jnp.bfloat16)
    own, partner = (from_near_ref[i, 0:1] + from_third_ref[i, 1:2] + both_ref[i, 2:3] for i in (0, 1))
    pair = jnp.abs(own - partner) + 0.5 * (own + partner)
    lane = lax.broadcasted_iota(jnp.int32, pair.shape, 1)
    for s in range(pair_ref.shape[0]):
        pair_ref[s] = jnp.sum(jnp.where(lane == s, pair, 0.0))


def local_call(kernel, name, out_shape, *xs, out_specs=None):
    return pl.pallas_call(
        kernel,
        out_shape=out_shape,
        in_specs=[VMEM] * len(xs),
        out_specs=out_specs or [VMEM] * len(out_shape),
        compiler_params=pltpu.CompilerParams(vmem_limit_bytes=16 * MIB),
        name=name,
    )(*map(near_memory, xs))


def send(x, route):
    return lax.ppermute(x, "expert", route)


def body(tokens, expert_ids, gate_fixed, scorer_id, direction_tags, w_gate, w_up, w_down, score_head):
    devices = lax.axis_size("expert")
    chips = devices // 2
    experts = w_gate.shape[0] * devices
    rows, width = tokens.shape
    x = pl.pallas_call(
        functools.partial(prep_kernel, experts),
        out_shape=pltpu.VMEM((rows, width + META), jnp.bfloat16),
        in_specs=[VMEM, VMEM, VMEM, SMEM, VMEM],
        out_specs=VMEM,
        name="prep",
    )(tokens, expert_ids.T, gate_fixed.T, scorer_id, direction_tags)
    weights = load(x, w_gate, w_up, w_down)

    def exchange(block, k):
        return send(block, [(d, d ^ (2 * k)) for d in range(devices)])

    def core_swap(block):
        return send(block, [(d, d ^ 1) for d in range(devices)])

    def pair(block):
        return block, core_swap(block)

    def partner_of(block):
        count = lax.axis_size("dp")
        return lax.ppermute(block, "dp", [(d, d ^ (count // 2)) for d in range(count)])

    def chip_sum(sums, dtype=jnp.bfloat16):
        same, other = sums
        return (same.astype(jnp.float32) + core_swap(other).astype(jnp.float32)).astype(dtype)

    def chip_route(*pairs):
        return [(2 * a + c, 2 * b + c) for a, b in pairs for c in (0, 1)]

    if chips == 4:
        far = exchange(x, 2)
        near = exchange(x, 1)
        near, far, x, *weights = lax.optimization_barrier((near, far, x, *weights))
        third = exchange(far, 1)
        far_sums, near_sums = ffn("experts_far_near", [pair(far), pair(near)], experts, weights)
        far_back = chip_sum(far_sums)
        relayed = send(far_back, chip_route((1, 3), (2, 0), (0, 1), (3, 2)))
        third_sums, own_sums = ffn("experts_third_own", [pair(third), pair(x)], experts, weights)
        near_back = chip_sum(near_sums)
        third_same, near_back = lax.optimization_barrier((third_sums[0], near_back))
        near = exchange(near_back, 1)
        (third_back,) = local_call(
            third_kernel, "third_back", [pltpu.VMEM((rows, width), jnp.bfloat16)], chip_sum((third_same, third_sums[1]), jnp.float32), relayed
        )
        third = exchange(third_back, 3)
        scores = (8, META)
        own_sum, score = local_call(
            own_kernel,
            "own_sum",
            [pltpu.VMEM((rows, width), jnp.float32), pltpu.VMEM(scores, jnp.float32)],
            *(own_sums[0], core_swap(own_sums[1]), relayed, near_back, third_back, score_head.reshape(1, width)),
        )
        (both,) = local_call(
            both_kernel, "both_scores", [pltpu.VMEM((2, *scores), jnp.float32)], score, partner_of(score)
        )
        return local_call(
            last_kernel,
            "mixed",
            [
                jax.ShapeDtypeStruct((rows, width), jnp.bfloat16),
                jax.ShapeDtypeStruct((rows // SEQ_LEN,), jnp.float32),
            ],
            own_sum,
            near,
            third,
            both,
            exchange(both, 1),
            exchange(both, 3),
            out_specs=[VMEM, SMEM],
        )
    held = [x] + [exchange(x, k) for k in range(1, chips)]
    sums = ffn("experts", [pair(b) for b in held], experts, weights)
    parts = [chip_sum(sums[0])] + [exchange(chip_sum(sums[k]), k) for k in range(1, chips)]
    mixed, seq_score = pl.pallas_call(
        functools.partial(finish_kernel, len(parts)),
        out_shape=(
            jax.ShapeDtypeStruct((rows, width), jnp.bfloat16),
            jax.ShapeDtypeStruct((rows // SEQ_LEN,), jnp.float32),
        ),
        in_specs=[VMEM] * len(parts) + [VMEM],
        out_specs=(VMEM, SMEM),
        name="finish",
    )(*parts, score_head.reshape(1, width))
    partner = partner_of(seq_score)
    pair_score = jnp.abs(seq_score - partner) + 0.5 * (seq_score + partner)
    return mixed, pair_score


def solution(mesh):
    tokens, whole = P(("dp", "expert"), None), P()
    weights = P("expert", None, None)
    return jax.shard_map(
        body,
        mesh=mesh,
        in_specs=(tokens, tokens, tokens, P(("dp", "expert")), whole, weights, weights, weights, whole),
        out_specs=(tokens, P(("dp", "expert"))),
        check_vma=False,
    )
```

```python
import functools

import jax
import jax.numpy as jnp
from jax import lax
from jax.experimental import pallas as pl
from jax.experimental.pallas import tpu as pltpu
from jax.sharding import PartitionSpec as P

SEQ_LEN = 16
MOST = 24
META = 128
MIB = 1 << 20

VMEM = pl.BlockSpec(memory_space=pltpu.VMEM)
SMEM = pl.BlockSpec(memory_space=pltpu.SMEM)
HBM = pl.BlockSpec(memory_space=pltpu.HBM)


def prep_kernel(experts, tok_ref, ids_ref, gate_ref, scorer_ref, tags_ref, out_ref):
    rows, width = tok_ref.shape
    for s in range(rows // SEQ_LEN):
        span = pl.ds(s * SEQ_LEN, SEQ_LEN)
        tag = jnp.where(scorer_ref[s] == 1, tags_ref[1:2, :], tags_ref[0:1, :]).astype(jnp.float32)
        out_ref[span, 0:width] = (tok_ref[span, :].astype(jnp.float32) + tag).astype(jnp.bfloat16)
    fixed = gate_ref[...].astype(jnp.float32)
    weight = fixed / jnp.sum(fixed, axis=0, keepdims=True)
    high = weight.astype(jnp.bfloat16).astype(jnp.float32)
    low = weight - high
    ids = ids_ref[...]
    place = lax.broadcasted_iota(jnp.int32, (META, rows), 0)
    meta = jnp.zeros((META, rows), jnp.float32)
    for k in range(ids.shape[0]):
        one = ids[k : k + 1, :]
        meta = meta + jnp.where(place == one, high[k : k + 1, :], 0.0)
        meta = meta + jnp.where(place == one + experts, low[k : k + 1, :], 0.0)
    out_ref[:, width : width + META] = meta.T.astype(jnp.bfloat16)


def pick_rows(meta, first, per_device, experts):
    rows = meta.shape[0]
    room = 2 * MOST
    lane = lax.broadcasted_iota(jnp.int32, meta.shape, 1)
    routed = (meta > 0) & (lane < experts)
    row = lax.broadcasted_iota(jnp.int32, (rows, rows), 0)
    col = lax.broadcasted_iota(jnp.int32, (rows, rows), 1)
    earlier = (row > col).astype(jnp.bfloat16)
    rank = jnp.dot(earlier, routed.astype(jnp.bfloat16), preferred_element_type=jnp.float32)
    rank = jnp.where(routed, rank, -1.0)
    slot = lax.broadcasted_iota(jnp.int32, (rows, per_device * room), 1)
    hit = jnp.zeros((rows, per_device * room), jnp.bool_)
    for e in range(per_device):
        mine = jnp.max(jnp.where(lane == first + e, rank, -1.0), axis=1, keepdims=True).astype(jnp.int32)
        hit = hit | ((mine >= 0) & (slot == mine + e * room))
    return hit.astype(jnp.float32).astype(jnp.bfloat16)


def hidden_rows(x, weight, w_gate, w_up):
    gate = jnp.dot(x, w_gate, preferred_element_type=jnp.float32)
    up = jnp.dot(x, w_up, preferred_element_type=jnp.float32)
    return (gate / (1.0 + jnp.exp(-gate)) * up * weight).astype(jnp.bfloat16)


def expert_weight(meta, expert, experts):
    lane = lax.broadcasted_iota(jnp.int32, meta.shape, 1)
    mine = (lane == expert) | (lane == expert + experts)
    return jnp.sum(jnp.where(mine, meta, 0.0), axis=1, keepdims=True)


def all_rows_kernel(experts, *refs):
    x_refs, (wg, wu, wd), out_refs, (x_ref,) = refs[:2], refs[2:5], refs[5:7], refs[7:]
    per_device, width, ff = wg.shape
    rows = x_refs[0].shape[0]
    first = lax.axis_index("expert") * per_device
    for i, ref in enumerate(x_refs):
        x_ref[i * rows : (i + 1) * rows, :] = ref[...]
    meta = x_ref[:, width:].astype(jnp.float32)

    def hidden_of(e):
        return hidden_rows(x_ref[:, 0:width], expert_weight(meta, first + e, experts), wg[e], wu[e])

    out = 0.0
    hidden = hidden_of(0)
    for e in range(1, per_device):
        following = hidden_of(e)
        out = out + jnp.dot(hidden, wd[e - 1], preferred_element_type=jnp.float32)
        hidden = following
    out = out + jnp.dot(hidden, wd[per_device - 1], preferred_element_type=jnp.float32)
    for i, ref in enumerate(out_refs):
        ref[...] = out[i * rows : (i + 1) * rows].astype(jnp.bfloat16)


def picked_rows_kernel(chips, experts, *refs):
    x_refs, (wg, wu, wd), refs = refs[: 2 * chips], refs[2 * chips : 2 * chips + 3], refs[2 * chips + 3 :]
    out_refs, (g_ref, pick_ref, o_ref) = refs[: 2 * chips], refs[2 * chips :]
    per_device, width, ff = wg.shape
    room = 2 * MOST
    first = lax.axis_index("expert") * per_device
    if g_ref.shape[1] > chips * room:
        g_ref[:, chips * room :, :] = jnp.zeros_like(g_ref[:, chips * room :, :])
    for k in range(chips):
        x = jnp.concatenate([x_refs[2 * k][...], x_refs[2 * k + 1][...]], axis=0)
        pick = pick_rows(x[:, width:].astype(jnp.float32), first, per_device, experts)
        pick_ref[k] = pick
        picked = lax.dot_general(pick, x, (((0,), (0,)), ((), ())), preferred_element_type=jnp.float32)
        picked = picked.astype(jnp.bfloat16)
        for e in range(per_device):
            g_ref[e, k * room : (k + 1) * room, :] = picked[e * room : (e + 1) * room, :]

    def hidden_of(e):
        meta = g_ref[e, :, width:].astype(jnp.float32)
        return hidden_rows(g_ref[e, :, 0:width], expert_weight(meta, first + e, experts), wg[e], wu[e])

    def leave(e, hidden):
        out = jnp.dot(hidden, wd[e], preferred_element_type=jnp.float32).astype(jnp.bfloat16)
        for k in range(chips):
            o_ref[k, e * room : (e + 1) * room, :] = out[k * room : (k + 1) * room, :]

    hidden = hidden_of(0)
    for e in range(1, per_device):
        following = hidden_of(e)
        leave(e - 1, hidden)
        hidden = following
    leave(per_device - 1, hidden)
    for k in range(chips):
        rows = jnp.dot(pick_ref[k], o_ref[k], preferred_element_type=jnp.float32).astype(jnp.bfloat16)
        half = rows.shape[0] // 2
        out_refs[2 * k][...] = rows[:half]
        out_refs[2 * k + 1][...] = rows[half:]


def far_memory(x):
    return pltpu.with_memory_space_constraint(x, pltpu.HBM)


def load_kernel(x_ref, *refs):
    count = (len(refs) - 1) // 2
    sems = refs[-1]
    copies = []
    for j in range(count):
        for e in range(refs[j].shape[0]):
            copy = pltpu.make_async_copy(refs[j].at[e], refs[count + j].at[e], sems.at[j, e])
            copy.start()
            copies.append(copy)
    for copy in copies:
        copy.wait()


def load(after, *arrays):
    return pl.pallas_call(
        load_kernel,
        out_shape=[pltpu.VMEM(a.shape, a.dtype) for a in arrays],
        in_specs=[VMEM] + [HBM] * len(arrays),
        out_specs=[VMEM] * len(arrays),
        scratch_shapes=[pltpu.SemaphoreType.DMA((len(arrays), arrays[0].shape[0]))],
        compiler_params=pltpu.CompilerParams(vmem_limit_bytes=MIB),
        cost_estimate=pl.CostEstimate(
            flops=0, bytes_accessed=sum(a.size * a.dtype.itemsize for a in arrays), transcendentals=0
        ),
        name="load_weights",
    )(near_memory(after), *map(far_memory, arrays))


def near_memory(x):
    return pltpu.with_memory_space_constraint(x, pltpu.VMEM)


def ffn(name, sources, experts, weights):
    per_device, width, ff = weights[0].shape
    xs = [near_memory(x) for pair in sources for x in pair]
    rows = xs[0].shape[0]
    chips = len(sources)
    room = 2 * MOST
    if chips == 1:
        met = 2 * rows
        kernel = functools.partial(all_rows_kernel, experts)
        scratch = [pltpu.VMEM((met, width + META), jnp.bfloat16)]
    else:
        met = -(-chips * room // META) * META
        kernel = functools.partial(picked_rows_kernel, chips, experts)
        scratch = [
            pltpu.VMEM((per_device, met, width + META), jnp.bfloat16),
            pltpu.VMEM((chips, 2 * rows, per_device * room), jnp.bfloat16),
            pltpu.VMEM((chips, per_device * room, width), jnp.bfloat16),
        ]
    outs = pl.pallas_call(
        kernel,
        out_shape=[pltpu.VMEM((rows, width), jnp.bfloat16)] * (2 * chips),
        in_specs=[VMEM] * (len(xs) + 3),
        out_specs=[VMEM] * (2 * chips),
        scratch_shapes=scratch,
        compiler_params=pltpu.CompilerParams(vmem_limit_bytes=16 * MIB),
        cost_estimate=pl.CostEstimate(
            flops=6 * per_device * met * width * ff,
            bytes_accessed=6 * per_device * width * ff,
            transcendentals=0,
        ),
        name=name,
    )(*xs, *map(near_memory, weights))
    return [(outs[2 * k], outs[2 * k + 1]) for k in range(chips)]


def finish_kernel(n_parts, *refs):
    parts, head_ref, mixed_ref, score_ref = refs[:n_parts], *refs[n_parts:]
    rows = mixed_ref.shape[0]
    total = parts[0][...].astype(jnp.float32)
    for part in parts[1:]:
        total = total + part[...].astype(jnp.float32)
    mixed = total.astype(jnp.bfloat16)
    mixed_ref[...] = mixed
    for s, score in enumerate(sequence_scores(mixed, head_ref[...])):
        score_ref[s] = score


def sequence_scores(rows, head):
    scored = rows.astype(jnp.float32) * head
    return [jnp.sum(scored[at : at + SEQ_LEN, :]) for at in range(0, rows.shape[0], SEQ_LEN)]


def score_tile(tile, row, rows, head):
    at = lax.broadcasted_iota(jnp.int32, tile.shape, 0)
    lane = lax.broadcasted_iota(jnp.int32, tile.shape, 1)
    for s, score in enumerate(sequence_scores(rows, head)):
        tile = jnp.where((at == row) & (lane == s), score, tile)
    return tile


def third_kernel(sum_ref, relayed_ref, back_ref):
    back_ref[...] = (sum_ref[...] + relayed_ref[...].astype(jnp.float32)).astype(jnp.bfloat16)


def own_kernel(own_ref, swapped_ref, near_ref, third_ref, head_ref, sum_ref, score_ref):
    own = own_ref[...].astype(jnp.float32) + swapped_ref[...].astype(jnp.float32)
    sum_ref[...] = own
    head = head_ref[...]
    tile = jnp.zeros(score_ref.shape, jnp.float32)
    for row, value in enumerate((near_ref[...], third_ref[...], own)):
        tile = score_tile(tile, row, value, head)
    score_ref[...] = tile


def both_kernel(score_ref, partner_ref, both_ref):
    both_ref[0] = score_ref[...]
    both_ref[1] = partner_ref[...]


def last_kernel(sum_ref, near_ref, third_ref, both_ref, from_near_ref, from_third_ref, mixed_ref, pair_ref):
    total = sum_ref[...] + near_ref[...].astype(jnp.float32) + third_ref[...].astype(jnp.float32)
    mixed_ref[...] = total.astype(jnp.bfloat16)
    own, partner = (from_near_ref[i, 0:1] + from_third_ref[i, 1:2] + both_ref[i, 2:3] for i in (0, 1))
    pair = jnp.abs(own - partner) + 0.5 * (own + partner)
    lane = lax.broadcasted_iota(jnp.int32, pair.shape, 1)
    for s in range(pair_ref.shape[0]):
        pair_ref[s] = jnp.sum(jnp.where(lane == s, pair, 0.0))


def local_call(kernel, name, out_shape, *xs, out_specs=None):
    return pl.pallas_call(
        kernel,
        out_shape=out_shape,
        in_specs=[VMEM] * len(xs),
        out_specs=out_specs or [VMEM] * len(out_shape),
        compiler_params=pltpu.CompilerParams(vmem_limit_bytes=16 * MIB),
        name=name,
    )(*map(near_memory, xs))


def send(x, route):
    return lax.ppermute(x, "expert", route)


def body(tokens, expert_ids, gate_fixed, scorer_id, direction_tags, w_gate, w_up, w_down, score_head):
    devices = lax.axis_size("expert")
    chips = devices // 2
    experts = w_gate.shape[0] * devices
    rows, width = tokens.shape
    x = pl.pallas_call(
        functools.partial(prep_kernel, experts),
        out_shape=pltpu.VMEM((rows, width + META), jnp.bfloat16),
        in_specs=[VMEM, VMEM, VMEM, SMEM, VMEM],
        out_specs=VMEM,
        name="prep",
    )(tokens, expert_ids.T, gate_fixed.T, scorer_id, direction_tags)
    weights = load(x, w_gate, w_up, w_down)

    def exchange(block, k):
        return send(block, [(d, d ^ (2 * k)) for d in range(devices)])

    def core_swap(block):
        return send(block, [(d, d ^ 1) for d in range(devices)])

    def pair(block):
        return block, core_swap(block)

    def partner_of(block):
        count = lax.axis_size("dp")
        return lax.ppermute(block, "dp", [(d, d ^ (count // 2)) for d in range(count)])

    def chip_sum(sums, dtype=jnp.bfloat16):
        same, other = sums
        return (same.astype(jnp.float32) + core_swap(other).astype(jnp.float32)).astype(dtype)

    if chips == 4:
        far = exchange(x, 2)
        near = exchange(x, 1)
        (own_sums,) = ffn("experts_own", [pair(x)], experts, weights)
        near, far, own_sums, *weights = lax.optimization_barrier((near, far, own_sums, *weights))
        third = exchange(far, 1)
        far_sums, near_sums = ffn("experts_far_near", [pair(far), pair(near)], experts, weights)
        far_back = chip_sum(far_sums)
        relayed = exchange(far_back, 1)
        (third_sums,) = ffn("experts_third", [pair(third)], experts, weights)
        near_back = chip_sum(near_sums)
        third_same, near_back = lax.optimization_barrier((third_sums[0], near_back))
        near = exchange(near_back, 1)
        (third_back,) = local_call(
            third_kernel, "third_back", [pltpu.VMEM((rows, width), jnp.bfloat16)], chip_sum((third_same, third_sums[1]), jnp.float32), relayed
        )
        third = exchange(third_back, 3)
        scores = (8, META)
        own_sum, score = local_call(
            own_kernel,
            "own_sum",
            [pltpu.VMEM((rows, width), jnp.float32), pltpu.VMEM(scores, jnp.float32)],
            *(own_sums[0], core_swap(own_sums[1]), near_back, third_back, score_head.reshape(1, width)),
        )
        (both,) = local_call(
            both_kernel, "both_scores", [pltpu.VMEM((2, *scores), jnp.float32)], score, partner_of(score)
        )
        return local_call(
            last_kernel,
            "mixed",
            [
                jax.ShapeDtypeStruct((rows, width), jnp.bfloat16),
                jax.ShapeDtypeStruct((rows // SEQ_LEN,), jnp.float32),
            ],
            own_sum,
            near,
            third,
            both,
            exchange(both, 1),
            exchange(both, 3),
            out_specs=[VMEM, SMEM],
        )
    held = [x] + [exchange(x, k) for k in range(1, chips)]
    sums = ffn("experts", [pair(b) for b in held], experts, weights)
    parts = [chip_sum(sums[0])] + [exchange(chip_sum(sums[k]), k) for k in range(1, chips)]
    mixed, seq_score = pl.pallas_call(
        functools.partial(finish_kernel, len(parts)),
        out_shape=(
            jax.ShapeDtypeStruct((rows, width), jnp.bfloat16),
            jax.ShapeDtypeStruct((rows // SEQ_LEN,), jnp.float32),
        ),
        in_specs=[VMEM] * len(parts) + [VMEM],
        out_specs=(VMEM, SMEM),
        name="finish",
    )(*parts, score_head.reshape(1, width))
    partner = partner_of(seq_score)
    pair_score = jnp.abs(seq_score - partner) + 0.5 * (seq_score + partner)
    return mixed, pair_score


def solution(mesh):
    tokens, whole = P(("dp", "expert"), None), P()
    weights = P("expert", None, None)
    return jax.shard_map(
        body,
        mesh=mesh,
        in_specs=(tokens, tokens, tokens, P(("dp", "expert")), whole, weights, weights, weights, whole),
        out_specs=(tokens, P(("dp", "expert"))),
        check_vma=False,
    )
```

```python
import functools

import jax
import jax.numpy as jnp
from jax import lax
from jax.experimental import pallas as pl
from jax.experimental.pallas import tpu as pltpu
from jax.sharding import PartitionSpec as P

SEQ_LEN = 16
MOST = 24
META = 128
MIB = 1 << 20

VMEM = pl.BlockSpec(memory_space=pltpu.VMEM)
SMEM = pl.BlockSpec(memory_space=pltpu.SMEM)
HBM = pl.BlockSpec(memory_space=pltpu.HBM)


def prep_kernel(experts, tok_ref, ids_ref, gate_ref, scorer_ref, tags_ref, out_ref):
    rows, width = tok_ref.shape
    for s in range(rows // SEQ_LEN):
        span = pl.ds(s * SEQ_LEN, SEQ_LEN)
        tag = jnp.where(scorer_ref[s] == 1, tags_ref[1:2, :], tags_ref[0:1, :]).astype(jnp.float32)
        out_ref[span, 0:width] = (tok_ref[span, :].astype(jnp.float32) + tag).astype(jnp.bfloat16)
    fixed = gate_ref[...].astype(jnp.float32)
    weight = fixed / jnp.sum(fixed, axis=0, keepdims=True)
    high = weight.astype(jnp.bfloat16).astype(jnp.float32)
    low = weight - high
    ids = ids_ref[...]
    place = lax.broadcasted_iota(jnp.int32, (META, rows), 0)
    meta = jnp.zeros((META, rows), jnp.float32)
    for k in range(ids.shape[0]):
        one = ids[k : k + 1, :]
        meta = meta + jnp.where(place == one, high[k : k + 1, :], 0.0)
        meta = meta + jnp.where(place == one + experts, low[k : k + 1, :], 0.0)
    out_ref[:, width : width + META] = meta.T.astype(jnp.bfloat16)


def pick_rows(meta, first, per_device, experts):
    rows = meta.shape[0]
    room = 2 * MOST
    lane = lax.broadcasted_iota(jnp.int32, meta.shape, 1)
    routed = (meta > 0) & (lane < experts)
    row = lax.broadcasted_iota(jnp.int32, (rows, rows), 0)
    col = lax.broadcasted_iota(jnp.int32, (rows, rows), 1)
    earlier = (row > col).astype(jnp.bfloat16)
    rank = jnp.dot(earlier, routed.astype(jnp.bfloat16), preferred_element_type=jnp.float32)
    rank = jnp.where(routed, rank, -1.0)
    slot = lax.broadcasted_iota(jnp.int32, (rows, per_device * room), 1)
    hit = jnp.zeros((rows, per_device * room), jnp.bool_)
    for e in range(per_device):
        mine = jnp.max(jnp.where(lane == first + e, rank, -1.0), axis=1, keepdims=True).astype(jnp.int32)
        hit = hit | ((mine >= 0) & (slot == mine + e * room))
    return hit.astype(jnp.float32).astype(jnp.bfloat16)


def hidden_rows(x, weight, w_gate, w_up):
    gate = jnp.dot(x, w_gate, preferred_element_type=jnp.float32)
    up = jnp.dot(x, w_up, preferred_element_type=jnp.float32)
    return (gate / (1.0 + jnp.exp(-gate)) * up * weight).astype(jnp.bfloat16)


def expert_weight(meta, expert, experts):
    lane = lax.broadcasted_iota(jnp.int32, meta.shape, 1)
    mine = (lane == expert) | (lane == expert + experts)
    return jnp.sum(jnp.where(mine, meta, 0.0), axis=1, keepdims=True)


def all_rows_kernel(experts, *refs):
    x_refs, (wg, wu, wd), out_refs, (x_ref,) = refs[:2], refs[2:5], refs[5:7], refs[7:]
    per_device, width, ff = wg.shape
    rows = x_refs[0].shape[0]
    first = lax.axis_index("expert") * per_device
    for i, ref in enumerate(x_refs):
        x_ref[i * rows : (i + 1) * rows, :] = ref[...]
    meta = x_ref[:, width:].astype(jnp.float32)

    def hidden_of(e):
        return hidden_rows(x_ref[:, 0:width], expert_weight(meta, first + e, experts), wg[e], wu[e])

    out = 0.0
    hidden = hidden_of(0)
    for e in range(1, per_device):
        following = hidden_of(e)
        out = out + jnp.dot(hidden, wd[e - 1], preferred_element_type=jnp.float32)
        hidden = following
    out = out + jnp.dot(hidden, wd[per_device - 1], preferred_element_type=jnp.float32)
    for i, ref in enumerate(out_refs):
        ref[...] = out[i * rows : (i + 1) * rows].astype(jnp.bfloat16)


def picked_rows_kernel(chips, experts, *refs):
    x_refs, (wg, wu, wd), refs = refs[: 2 * chips], refs[2 * chips : 2 * chips + 3], refs[2 * chips + 3 :]
    out_refs, (g_ref, pick_ref, o_ref) = refs[: 2 * chips], refs[2 * chips :]
    per_device, width, ff = wg.shape
    room = 2 * MOST
    first = lax.axis_index("expert") * per_device
    if g_ref.shape[1] > chips * room:
        g_ref[:, chips * room :, :] = jnp.zeros_like(g_ref[:, chips * room :, :])
    for k in range(chips):
        x = jnp.concatenate([x_refs[2 * k][...], x_refs[2 * k + 1][...]], axis=0)
        pick = pick_rows(x[:, width:].astype(jnp.float32), first, per_device, experts)
        pick_ref[k] = pick
        picked = lax.dot_general(pick, x, (((0,), (0,)), ((), ())), preferred_element_type=jnp.float32)
        picked = picked.astype(jnp.bfloat16)
        for e in range(per_device):
            g_ref[e, k * room : (k + 1) * room, :] = picked[e * room : (e + 1) * room, :]

    def hidden_of(e):
        meta = g_ref[e, :, width:].astype(jnp.float32)
        return hidden_rows(g_ref[e, :, 0:width], expert_weight(meta, first + e, experts), wg[e], wu[e])

    def leave(e, hidden):
        out = jnp.dot(hidden, wd[e], preferred_element_type=jnp.float32).astype(jnp.bfloat16)
        for k in range(chips):
            o_ref[k, e * room : (e + 1) * room, :] = out[k * room : (k + 1) * room, :]

    hidden = hidden_of(0)
    for e in range(1, per_device):
        following = hidden_of(e)
        leave(e - 1, hidden)
        hidden = following
    leave(per_device - 1, hidden)
    for k in range(chips):
        rows = jnp.dot(pick_ref[k], o_ref[k], preferred_element_type=jnp.float32).astype(jnp.bfloat16)
        half = rows.shape[0] // 2
        out_refs[2 * k][...] = rows[:half]
        out_refs[2 * k + 1][...] = rows[half:]


def far_memory(x):
    return pltpu.with_memory_space_constraint(x, pltpu.HBM)


def load_kernel(x_ref, *refs):
    count = (len(refs) - 1) // 2
    sems = refs[-1]
    copies = []
    for j in range(count):
        for e in range(refs[j].shape[0]):
            copy = pltpu.make_async_copy(refs[j].at[e], refs[count + j].at[e], sems.at[j, e])
            copy.start()
            copies.append(copy)
    for copy in copies:
        copy.wait()


def load(after, *arrays):
    return pl.pallas_call(
        load_kernel,
        out_shape=[pltpu.VMEM(a.shape, a.dtype) for a in arrays],
        in_specs=[VMEM] + [HBM] * len(arrays),
        out_specs=[VMEM] * len(arrays),
        scratch_shapes=[pltpu.SemaphoreType.DMA((len(arrays), arrays[0].shape[0]))],
        compiler_params=pltpu.CompilerParams(vmem_limit_bytes=MIB),
        cost_estimate=pl.CostEstimate(
            flops=0, bytes_accessed=sum(a.size * a.dtype.itemsize for a in arrays), transcendentals=0
        ),
        name="load_weights",
    )(near_memory(after), *map(far_memory, arrays))


def near_memory(x):
    return pltpu.with_memory_space_constraint(x, pltpu.VMEM)


def ffn(name, sources, experts, weights):
    per_device, width, ff = weights[0].shape
    xs = [near_memory(x) for pair in sources for x in pair]
    rows = xs[0].shape[0]
    chips = len(sources)
    room = 2 * MOST
    if chips == 1:
        met = 2 * rows
        kernel = functools.partial(all_rows_kernel, experts)
        scratch = [pltpu.VMEM((met, width + META), jnp.bfloat16)]
    else:
        met = max(META, -(-chips * room // 32) * 32)
        kernel = functools.partial(picked_rows_kernel, chips, experts)
        scratch = [
            pltpu.VMEM((per_device, met, width + META), jnp.bfloat16),
            pltpu.VMEM((chips, 2 * rows, per_device * room), jnp.bfloat16),
            pltpu.VMEM((chips, per_device * room, width), jnp.bfloat16),
        ]
    outs = pl.pallas_call(
        kernel,
        out_shape=[pltpu.VMEM((rows, width), jnp.bfloat16)] * (2 * chips),
        in_specs=[VMEM] * (len(xs) + 3),
        out_specs=[VMEM] * (2 * chips),
        scratch_shapes=scratch,
        compiler_params=pltpu.CompilerParams(vmem_limit_bytes=16 * MIB),
        cost_estimate=pl.CostEstimate(
            flops=6 * per_device * met * width * ff,
            bytes_accessed=6 * per_device * width * ff,
            transcendentals=0,
        ),
        name=name,
    )(*xs, *map(near_memory, weights))
    return [(outs[2 * k], outs[2 * k + 1]) for k in range(chips)]


def finish_kernel(n_parts, *refs):
    parts, head_ref, mixed_ref, score_ref = refs[:n_parts], *refs[n_parts:]
    rows = mixed_ref.shape[0]
    total = parts[0][...].astype(jnp.float32)
    for part in parts[1:]:
        total = total + part[...].astype(jnp.float32)
    mixed = total.astype(jnp.bfloat16)
    mixed_ref[...] = mixed
    for s, score in enumerate(sequence_scores(mixed, head_ref[...])):
        score_ref[s] = score


def sequence_scores(rows, head):
    scored = rows.astype(jnp.float32) * head
    return [jnp.sum(scored[at : at + SEQ_LEN, :]) for at in range(0, rows.shape[0], SEQ_LEN)]


def score_tile(tile, row, rows, head):
    at = lax.broadcasted_iota(jnp.int32, tile.shape, 0)
    lane = lax.broadcasted_iota(jnp.int32, tile.shape, 1)
    for s, score in enumerate(sequence_scores(rows, head)):
        tile = jnp.where((at == row) & (lane == s), score, tile)
    return tile


def third_kernel(sum_ref, relayed_ref, back_ref):
    back_ref[...] = (sum_ref[...] + relayed_ref[...].astype(jnp.float32)).astype(jnp.bfloat16)


def own_kernel(own_ref, swapped_ref, near_ref, third_ref, head_ref, sum_ref, score_ref):
    own = own_ref[...].astype(jnp.float32) + swapped_ref[...].astype(jnp.float32)
    sum_ref[...] = own
    head = head_ref[...]
    tile = jnp.zeros(score_ref.shape, jnp.float32)
    for row, value in enumerate((near_ref[...], third_ref[...], own)):
        tile = score_tile(tile, row, value, head)
    score_ref[...] = tile


def both_kernel(score_ref, partner_ref, both_ref):
    both_ref[0] = score_ref[...]
    both_ref[1] = partner_ref[...]


def last_kernel(sum_ref, near_ref, third_ref, both_ref, from_near_ref, from_third_ref, mixed_ref, pair_ref):
    total = sum_ref[...] + near_ref[...].astype(jnp.float32) + third_ref[...].astype(jnp.float32)
    mixed_ref[...] = total.astype(jnp.bfloat16)
    own, partner = (from_near_ref[i, 0:1] + from_third_ref[i, 1:2] + both_ref[i, 2:3] for i in (0, 1))
    pair = jnp.abs(own - partner) + 0.5 * (own + partner)
    lane = lax.broadcasted_iota(jnp.int32, pair.shape, 1)
    for s in range(pair_ref.shape[0]):
        pair_ref[s] = jnp.sum(jnp.where(lane == s, pair, 0.0))


def local_call(kernel, name, out_shape, *xs, out_specs=None):
    return pl.pallas_call(
        kernel,
        out_shape=out_shape,
        in_specs=[VMEM] * len(xs),
        out_specs=out_specs or [VMEM] * len(out_shape),
        compiler_params=pltpu.CompilerParams(vmem_limit_bytes=16 * MIB),
        name=name,
    )(*map(near_memory, xs))


def send(x, route):
    return lax.ppermute(x, "expert", route)


def body(tokens, expert_ids, gate_fixed, scorer_id, direction_tags, w_gate, w_up, w_down, score_head):
    devices = lax.axis_size("expert")
    chips = devices // 2
    experts = w_gate.shape[0] * devices
    rows, width = tokens.shape
    x = pl.pallas_call(
        functools.partial(prep_kernel, experts),
        out_shape=pltpu.VMEM((rows, width + META), jnp.bfloat16),
        in_specs=[VMEM, VMEM, VMEM, SMEM, VMEM],
        out_specs=VMEM,
        name="prep",
    )(tokens, expert_ids.T, gate_fixed.T, scorer_id, direction_tags)
    weights = load(x, w_gate, w_up, w_down)

    def exchange(block, k):
        return send(block, [(d, d ^ (2 * k)) for d in range(devices)])

    def core_swap(block):
        return send(block, [(d, d ^ 1) for d in range(devices)])

    def pair(block):
        return block, core_swap(block)

    def partner_of(block):
        count = lax.axis_size("dp")
        return lax.ppermute(block, "dp", [(d, d ^ (count // 2)) for d in range(count)])

    def chip_sum(sums, dtype=jnp.bfloat16):
        same, other = sums
        return (same.astype(jnp.float32) + core_swap(other).astype(jnp.float32)).astype(dtype)

    if chips == 4:
        far = exchange(x, 2)
        near = exchange(x, 1)
        x_pair = pair(x)
        far, near, x_pair, *weights = lax.optimization_barrier((far, near, x_pair, *weights))
        third = exchange(far, 1)
        far_sums, near_sums, own_sums = ffn("experts_first", [pair(far), pair(near), x_pair], experts, weights)
        far_back = chip_sum(far_sums)
        relayed = exchange(far_back, 1)
        (third_sums,) = ffn("experts_third", [pair(third)], experts, weights)
        near_back = chip_sum(near_sums)
        third_same, near_back = lax.optimization_barrier((third_sums[0], near_back))
        near = exchange(near_back, 1)
        (third_back,) = local_call(
            third_kernel, "third_back", [pltpu.VMEM((rows, width), jnp.bfloat16)], chip_sum((third_same, third_sums[1]), jnp.float32), relayed
        )
        third = exchange(third_back, 3)
        scores = (8, META)
        own_sum, score = local_call(
            own_kernel,
            "own_sum",
            [pltpu.VMEM((rows, width), jnp.float32), pltpu.VMEM(scores, jnp.float32)],
            *(own_sums[0], core_swap(own_sums[1]), near_back, third_back, score_head.reshape(1, width)),
        )
        (both,) = local_call(
            both_kernel, "both_scores", [pltpu.VMEM((2, *scores), jnp.float32)], score, partner_of(score)
        )
        return local_call(
            last_kernel,
            "mixed",
            [
                jax.ShapeDtypeStruct((rows, width), jnp.bfloat16),
                jax.ShapeDtypeStruct((rows // SEQ_LEN,), jnp.float32),
            ],
            own_sum,
            near,
            third,
            both,
            exchange(both, 1),
            exchange(both, 3),
            out_specs=[VMEM, SMEM],
        )
    held = [x] + [exchange(x, k) for k in range(1, chips)]
    sums = ffn("experts", [pair(b) for b in held], experts, weights)
    parts = [chip_sum(sums[0])] + [exchange(chip_sum(sums[k]), k) for k in range(1, chips)]
    mixed, seq_score = pl.pallas_call(
        functools.partial(finish_kernel, len(parts)),
        out_shape=(
            jax.ShapeDtypeStruct((rows, width), jnp.bfloat16),
            jax.ShapeDtypeStruct((rows // SEQ_LEN,), jnp.float32),
        ),
        in_specs=[VMEM] * len(parts) + [VMEM],
        out_specs=(VMEM, SMEM),
        name="finish",
    )(*parts, score_head.reshape(1, width))
    partner = partner_of(seq_score)
    pair_score = jnp.abs(seq_score - partner) + 0.5 * (seq_score + partner)
    return mixed, pair_score


def solution(mesh):
    tokens, whole = P(("dp", "expert"), None), P()
    weights = P("expert", None, None)
    return jax.shard_map(
        body,
        mesh=mesh,
        in_specs=(tokens, tokens, tokens, P(("dp", "expert")), whole, weights, weights, weights, whole),
        out_specs=(tokens, P(("dp", "expert"))),
        check_vma=False,
    )
```
